128 devices in a mesh: ctx: 8 (over z, x_lo), head: 8 (over y, x_hi), rep: 2 (over core).
Axes of the slice: x: 4 (x_hi: 2, x_lo: 2; x = x_hi * 2 + x_lo), y: 4, z: 4, core: 2. Of those that a mesh axis runs over, the one named last changes fastest.
Arguments:
- prefix_query: bfloat16 [8192, 64, 128], P(('ctx', 'rep'), 'head'), may hold values from -6 to 6
- prefix_kv: bfloat16 [8192, 8, 2, 128], P(('ctx', 'rep'), 'head'), may hold values from -6 to 6
- decode_query: bfloat16 [1024, 64, 128], P(('ctx', 'rep'), 'head'), may hold values from -6 to 6
- tail_key_value: bfloat16 [1024, 128, 8, 2, 128], P(('ctx', 'rep'), None, 'head'), may hold values from -6 to 6
- tail_len: int32 [1024], P(('ctx', 'rep')), may hold values from 1 to 128, as said below
- out_weight: bfloat16 [8192, 8192], P('head', ('ctx', 'rep')), may hold values from -0.0625 to 0.0625
Outputs:
- prefix_out: bfloat16 [8192, 64, 128], P(('ctx', 'rep'), 'head')
- decoded: bfloat16 [1024, 8192], P('head', ('ctx', 'rep'))
The draws below stay inside these ranges and needn't reach their ends.
Inputs may be any that keep to these rules, and one draw needn't show every extreme that they name: `tail_len`: the last of a rollout's own tokens is its new token; in each aligned block of 64 rollouts some rollout has exactly 128.
All inputs are finite; a program needn't handle non-finite values.
Results may differ from the reference program's by a relative error of at most 0.023.
Values may be sent and summed in bfloat16 or wider, within the bound.
A program may use at most 64 MiB of HBM per device.

```python
import jax
import jax.numpy as jnp
from jax import lax

QUERY_HEADS = 64
KEY_VALUE_HEADS = 8
HEAD_WIDTH = 128
D = 8192
SEQ_DEV = 512
ROLL_DEV = 64
TAIL_LENGTH = 128
PREFIX_LENGTH = 8192
ROLLOUT_COUNT = 1024


def draw_prefix_query(key, part):
    key = jax.random.fold_in(key, 12)
    gaussian_part = jnp.clip(jax.random.normal(key, (PREFIX_LENGTH, QUERY_HEADS, HEAD_WIDTH), jnp.float32), -6.0, 6.0)
    return gaussian_part.astype(jnp.bfloat16)


def draw_prefix_kv(key, part):
    key = jax.random.fold_in(key, 11)
    gaussian_part = jnp.clip(jax.random.normal(key, (PREFIX_LENGTH, KEY_VALUE_HEADS, 2, HEAD_WIDTH), jnp.float32), -6.0, 6.0)
    return gaussian_part.astype(jnp.bfloat16)


def draw_decode_query(key, part):
    key = jax.random.fold_in(key, 13)
    gaussian_part = jnp.clip(jax.random.normal(key, (ROLLOUT_COUNT, QUERY_HEADS, HEAD_WIDTH), jnp.float32), -6.0, 6.0)
    return gaussian_part.astype(jnp.bfloat16)


def draw_tail_len(key, part):
    key = jax.random.fold_in(key, 14)
    first_key, second_key = jax.random.split(key)
    lengths = jax.random.randint(first_key, (ROLLOUT_COUNT,), 1, TAIL_LENGTH + 1, dtype=jnp.int32)
    picked = jax.random.randint(second_key, (ROLLOUT_COUNT // ROLL_DEV,), 0, ROLL_DEV, dtype=jnp.int32)
    filled = jnp.arange(ROLLOUT_COUNT, dtype=jnp.int32) % ROLL_DEV == jnp.repeat(picked, ROLL_DEV)
    return jnp.where(filled, TAIL_LENGTH, lengths).astype(jnp.int32)


def block_scale(key, extent, cuts, smallest, largest):
    def one(dim, blocks):
        steps = jax.random.uniform(jax.random.fold_in(jax.random.fold_in(key, 6), dim), (blocks,), jnp.float32, smallest / len(cuts), largest / len(cuts))
        return jnp.repeat(jnp.exp(steps), extent[dim] // blocks).reshape((-1,) + (1,) * (len(extent) - dim - 1))

    loudness = one(*cuts[0])
    for cut in cuts[1:]:
        loudness = loudness * one(*cut)
    return loudness


def normal_values(rng, dims, scale, bound, cuts=(), held_as=jnp.bfloat16):
    loudness = block_scale(rng, dims, cuts, -0.22, 0.18) if cuts else 1.0
    result = jax.random.normal(rng, dims, jnp.float32) * scale * loudness
    return jnp.minimum(jnp.maximum(result, -bound), bound).astype(held_as)


def setup_inputs(seed: int = 0) -> dict:
    key_list = jax.random.split(jax.random.key(seed), 7)
    prefix_query = draw_prefix_query(jax.random.fold_in(key_list[6], 71), 0)
    prefix_kv = draw_prefix_kv(jax.random.fold_in(key_list[6], 71), 0)
    decode_query = draw_decode_query(jax.random.fold_in(key_list[6], 71), 0)
    tail_key_value = normal_values(key_list[3], (ROLLOUT_COUNT, TAIL_LENGTH, KEY_VALUE_HEADS, 2, HEAD_WIDTH), 1.0, 6.0, ((0, 16), (2, 8)))
    tail_len = draw_tail_len(jax.random.fold_in(key_list[6], 71), 0)
    out_weight = normal_values(key_list[5], (QUERY_HEADS * HEAD_WIDTH, D), (QUERY_HEADS * HEAD_WIDTH) ** -0.5, 0.0625, ((0, 8), (1, 16)))
    return {"prefix_query": prefix_query, "prefix_kv": prefix_kv, "decode_query": decode_query, "tail_key_value": tail_key_value, "tail_len": tail_len, "out_weight": out_weight}


LOW_FILL = -1e30


def rounded(weights):
    return lax.optimization_barrier(weights.astype(jnp.bfloat16)).astype(jnp.float32)


def prefix_group(operands):
    group_query, group_keys, group_values = operands
    score_scale = HEAD_WIDTH ** -0.5
    key_position = jnp.arange(PREFIX_LENGTH, dtype=jnp.int32)
    keys_wide = group_keys.astype(jnp.float32)
    values_wide = group_values.astype(jnp.float32)

    def one_block(block_index):
        block_query = lax.dynamic_slice_in_dim(group_query, block_index * SEQ_DEV, SEQ_DEV, 0).astype(jnp.float32)
        query_position = block_index * SEQ_DEV + jnp.arange(SEQ_DEV, dtype=jnp.int32)
        visible = (key_position[None, :] <= query_position[:, None])[:, None, :]
        scores = jnp.einsum("qgd,kd->qgk", block_query, keys_wide) * score_scale
        scores = jnp.where(visible, scores, LOW_FILL)
        row_max = jnp.max(scores, axis=-1)
        weights = jnp.where(visible, jnp.exp(scores - row_max[..., None]), 0.0)
        row_sum = jnp.sum(weights, axis=-1)
        mixed = jnp.einsum("qgk,kd->qgd", rounded(weights), values_wide)
        return (mixed / row_sum[..., None]).astype(jnp.bfloat16)

    block_list = lax.map(one_block, jnp.arange(PREFIX_LENGTH // SEQ_DEV, dtype=jnp.int32))
    return block_list.reshape(PREFIX_LENGTH, QUERY_HEADS // KEY_VALUE_HEADS, HEAD_WIDTH)


def reference(prefix_query, prefix_kv, decode_query, tail_key_value, tail_len, out_weight):
    group_width = QUERY_HEADS // KEY_VALUE_HEADS
    score_scale = HEAD_WIDTH ** -0.5
    query_grouping = prefix_query.reshape(PREFIX_LENGTH, KEY_VALUE_HEADS, group_width, HEAD_WIDTH).transpose(1, 0, 2, 3)
    key_groups = prefix_kv[:, :, 0, :].transpose(1, 0, 2)
    value_groups = prefix_kv[:, :, 1, :].transpose(1, 0, 2)
    prefix_out = lax.map(prefix_group, (query_grouping, key_groups, value_groups))
    prefix_out = prefix_out.transpose(1, 0, 2, 3).reshape(PREFIX_LENGTH, QUERY_HEADS, HEAD_WIDTH)

    rollout_groups = decode_query.reshape(ROLLOUT_COUNT, KEY_VALUE_HEADS, group_width, HEAD_WIDTH).transpose(1, 0, 2, 3)
    own_key_groups = tail_key_value[:, :, :, 0, :].transpose(2, 0, 1, 3)
    own_value_groups = tail_key_value[:, :, :, 1, :].transpose(2, 0, 1, 3)
    tail_visible = (jnp.arange(TAIL_LENGTH, dtype=jnp.int32)[None, :] < tail_len[:, None])[:, None, :]

    def decode_group(operands):
        group_query, group_keys, group_values, own_keys, own_values = operands
        query_wide = group_query.astype(jnp.float32)
        prefix_scores = jnp.einsum("rgd,kd->rgk", query_wide, group_keys.astype(jnp.float32)) * score_scale
        own_scores = jnp.einsum("rgd,rtd->rgt", query_wide, own_keys.astype(jnp.float32)) * score_scale
        own_scores = jnp.where(tail_visible, own_scores, LOW_FILL)
        row_max = jnp.maximum(jnp.max(prefix_scores, axis=-1), jnp.max(own_scores, axis=-1))
        prefix_weights = jnp.exp(prefix_scores - row_max[..., None])
        own_weights = jnp.where(tail_visible, jnp.exp(own_scores - row_max[..., None]), 0.0)
        row_sum = jnp.sum(prefix_weights, axis=-1) + jnp.sum(own_weights, axis=-1)
        mixed = jnp.einsum("rgk,kd->rgd", rounded(prefix_weights), group_values.astype(jnp.float32))
        mixed = mixed + jnp.einsum("rgt,rtd->rgd", rounded(own_weights), own_values.astype(jnp.float32))
        return (mixed / row_sum[..., None]).astype(jnp.bfloat16)

    attended = lax.map(decode_group, (rollout_groups, key_groups, value_groups, own_key_groups, own_value_groups))
    attended = attended.transpose(1, 0, 2, 3).reshape(ROLLOUT_COUNT, QUERY_HEADS * HEAD_WIDTH)
    decoded = jnp.dot(attended, out_weight, preferred_element_type=jnp.float32).astype(jnp.bfloat16)
    return prefix_out, decoded
```

```python
import functools

import jax
import jax.numpy as jnp
from jax import lax
from jax.experimental import pallas as pl
from jax.experimental.pallas import tpu as pltpu
from jax.sharding import PartitionSpec as P

F32, BF16 = jnp.float32, jnp.bfloat16
MESH = pl.DeviceIdType.MESH
LOW_FILL = -1e30
WIDTH = 128
SCALE = WIDTH**-0.5 * 1.4426950408889634
BLOCK = 512
CHUNK = 512
CHUNKS = 8
GUESTS = 4
SLOTS = 1 + CHUNKS + GUESTS
NT = (((1,), (1,)), ((), ()))


def wide(column, width):
    return jnp.concatenate([column] * (width // WIDTH), axis=1)


def kernel(
    q_hbm, kv_hbm, dq_hbm, tail_hbm, len_ref, w_hbm,
    out_hbm, dec_ref,
    kvint, kbuf, vbuf, qbuf, tailbuf, wbuf, m_ref, l_ref, acc_ref,
    obuf, fbuf, att, part, landed,
    in_sem, q_sem, send_sem, kv_sem, att_sem, guest_sem, back_sem, rs_sem, out_sem,
):
    ctx, head, rep = lax.axis_index("ctx"), lax.axis_index("head"), lax.axis_index("rep")
    z, x = ctx // 2, ctx % 2
    me = ctx * 2 + rep
    mate = 15 - me
    late = me >= 8
    guests = jnp.where(late, 0, mate // 2 - 3)
    given = jnp.where(late, me // 2 - 3, 0)
    own_base = 1 + guests
    own_count = CHUNKS - given

    def place(dz, flip):
        return ((z + dz) % 4) * 2 + (1 - x if flip else x)

    chips = [ctx, place(0, True), place(1, False), place(3, False),
             place(1, True), place(3, True), place(2, False), place(2, True)]
    OWN, XP, ZP, ZM, ZPX, ZMX, ZZ, ZZX = range(8)

    sibling = {"ctx": ctx, "rep": 1 - rep}
    over_x = {"ctx": chips[XP], "rep": rep}
    over_zp = {"ctx": chips[ZP], "rep": rep}
    over_zm = {"ctx": chips[ZM], "rep": rep}
    to_mate = {"ctx": mate // 2, "rep": mate % 2}

    def load(src, dst, sem):
        copy = pltpu.make_async_copy(src, dst, sem)
        copy.start()
        return copy

    kv_in = load(kv_hbm, kvint, in_sem.at[0])
    dq_in = load(dq_hbm, qbuf.at[pl.ds(0, CHUNK)], in_sem.at[1])

    def own_q(k):
        return pltpu.make_async_copy(
            q_hbm.at[pl.ds(pl.multiple_of((given + k) * CHUNK, CHUNK), CHUNK)],
            qbuf.at[pl.ds(pl.multiple_of((own_base + k) * CHUNK, CHUNK), CHUNK)],
            q_sem.at[k],
        )

    for k in range(CHUNKS):
        @pl.when(k < own_count)
        def _(k=k):
            own_q(k).start()

    tail_in = load(tail_hbm, tailbuf, in_sem.at[2])
    w_in = load(w_hbm, wbuf, in_sem.at[3])

    barrier = pltpu.get_barrier_semaphore()
    for device in (sibling, over_x, over_zp, over_zm, to_mate):
        pl.semaphore_signal(barrier, inc=1, device_id=device, device_id_type=MESH)
    for away in range(1, 8):
        pl.semaphore_signal(
            barrier, inc=1, device_id={"head": (head + away) % 8}, device_id_type=MESH
        )

    rows = lax.broadcasted_iota(jnp.int32, (256, 256), 0)
    cols = lax.broadcasted_iota(jnp.int32, (256, 256), 1)
    wanted = jnp.where(rows < 128, rows * 2, (rows - 128) * 2 + 1)
    pick = jnp.where(cols == wanted, 1.0, 0.0).astype(BF16)
    kv_in.wait()
    for t in range(4):
        apart = jnp.dot(pick, kvint[t * 256:(t + 1) * 256, :], preferred_element_type=F32)
        apart = apart.astype(BF16)
        here = pl.ds(pl.multiple_of(me * BLOCK + t * 128, 128), 128)
        kbuf[here, :] = apart[:128]
        vbuf[here, :] = apart[128:]

    pl.semaphore_wait(barrier, 12)

    sends = []

    def block_of(which, s, kind, piece):
        b = chips[s] * 2 + (rep if kind == 0 else 1 - rep)
        if which == "kv":
            ref = kbuf if piece == 0 else vbuf
            return ref.at[pl.ds(pl.multiple_of(b * BLOCK, BLOCK), BLOCK)]
        return att.at[pl.ds(pl.multiple_of(b * 64 + piece * 32, 32), 32)]

    def sem_of(which):
        return kv_sem if which == "kv" else att_sem

    def send(which, s, piece, device, s_there, kind_there):
        copy = pltpu.make_async_remote_copy(
            src_ref=block_of(which, s, 0, piece),
            dst_ref=block_of(which, s, 0, piece),
            send_sem=send_sem.at[len(sends)],
            recv_sem=sem_of(which).at[s_there, kind_there, piece],
            device_id=device,
            device_id_type=MESH,
        )
        copy.start()
        sends.append(copy)

    def arrived(which, s, kind, pieces=(0, 1)):
        for piece in pieces:
            ref = block_of(which, s, kind, piece)
            pltpu.make_async_remote_copy(
                src_ref=ref, dst_ref=ref, send_sem=send_sem.at[0],
                recv_sem=sem_of(which).at[s, kind, piece],
                device_id=sibling, device_id_type=MESH,
            ).wait_recv()

    def both(which, s, device, s_there, kind_there):
        for piece in (0, 1):
            send(which, s, piece, device, s_there, kind_there)

    def gather_start(which):
        both(which, OWN, over_zp, ZM, 0)
        both(which, OWN, over_zm, ZP, 0)
        both(which, OWN, over_x, XP, 0)
        both(which, OWN, sibling, OWN, 1)

    def gather_first(which):
        arrived(which, XP, 0)
        both(which, XP, over_zp, ZMX, 0)
        both(which, XP, over_zm, ZPX, 0)
        both(which, XP, sibling, XP, 1)
        arrived(which, ZM, 0)
        send(which, ZM, 0, over_zp, ZZ, 0)
        both(which, ZM, sibling, ZM, 1)
        arrived(which, ZP, 0)
        send(which, ZP, 1, over_zm, ZZ, 0)
        both(which, ZP, sibling, ZP, 1)

    def gather_second(which):
        arrived(which, ZMX, 0)
        send(which, ZMX, 0, over_zp, ZZX, 0)
        both(which, ZMX, sibling, ZMX, 1)
        arrived(which, ZPX, 0)
        send(which, ZPX, 1, over_zm, ZZX, 0)
        both(which, ZPX, sibling, ZPX, 1)

    def gather_third(which):
        arrived(which, ZZ, 0)
        both(which, ZZ, sibling, ZZ, 1)
        arrived(which, ZZX, 0)
        both(which, ZZX, sibling, ZZX, 1)

    gather_start("kv")

    def guest_q(k):
        return pltpu.make_async_remote_copy(
            src_ref=q_hbm.at[pl.ds(k * CHUNK, CHUNK)],
            dst_ref=qbuf.at[pl.ds((1 + k) * CHUNK, CHUNK)],
            send_sem=guest_sem.at[0, k], recv_sem=guest_sem.at[1, k],
            device_id=to_mate, device_id_type=MESH,
        )

    for k in range(GUESTS):
        @pl.when(k < given)
        def _(k=k):
            guest_q(k).start()

    def rows_of(slot):
        return pl.ds(pl.multiple_of(slot * CHUNK, CHUNK), CHUNK)

    def absorb(slots, first_key, keys, first_place=None):
        key_rows = pl.ds(pl.multiple_of(first_key, keys), keys)
        where = [rows_of(slot) for slot in slots]
        m_old = [m_ref[r, :] for r in where]
        l_old = [l_ref[r, :] for r in where]
        a_old = [acc_ref[r, :] for r in where]
        scores = [
            lax.dot_general(qbuf[r, :], kbuf[key_rows, :], NT, preferred_element_type=F32)
            for r in where
        ]
        result = []
        for i in range(len(slots)):
            s = scores[i]
            if first_place is not None:
                row = lax.broadcasted_iota(jnp.int32, s.shape, 0) // 8 + first_place[i]
                s = jnp.where(lax.broadcasted_iota(jnp.int32, s.shape, 1) <= row, s, LOW_FILL)
            m_new = jnp.maximum(m_old[i], jnp.max(s, axis=1, keepdims=True))
            p = jnp.exp2((s - wide(m_new, keys)) * SCALE)
            factor = jnp.exp2((m_old[i] - m_new) * SCALE)
            total = p[:, :WIDTH]
            for j in range(1, keys // WIDTH):
                total = total + p[:, j * WIDTH:(j + 1) * WIDTH]
            mixed = jnp.dot(p.astype(BF16), vbuf[key_rows, :], preferred_element_type=F32)
            result.append((m_new, l_old[i] * factor + total, a_old[i] * factor + mixed))
        for i, r in enumerate(where):
            m_ref[r, :], l_ref[r, :], acc_ref[r, :] = result[i]

    def sweep(first, count, first_key, keys, place=None):
        def at(slot):
            return None if place is None else [(s - first + place) * 64 for s in slot]

        def pair(t, _):
            slots = [first + 2 * t, first + 2 * t + 1]
            absorb(slots, first_key, keys, at(slots))
            return 0

        lax.fori_loop(0, count // 2, pair, 0)

        @pl.when(count % 2 == 1)
        def _():
            slots = [first + count - 1]
            absorb(slots, first_key, keys, at(slots))

    def others(chip):
        mine = jnp.where(chip < me // 2, own_count, 0)
        theirs = jnp.where(jnp.logical_and(jnp.logical_not(late), chip < mate // 2), guests, 0)
        return mine + theirs

    def both_blocks(chip):
        sweep(1, others(chip), chip * 2 * BLOCK, 2 * BLOCK)

    def decode_step(chip):
        absorb([0], chip * 2 * BLOCK, 2 * BLOCK)

    m_ref[CHUNK:, :] = jnp.full((CHUNK * (SLOTS - 1), WIDTH), LOW_FILL, F32)
    l_ref[CHUNK:, :] = jnp.zeros((CHUNK * (SLOTS - 1), WIDTH), F32)
    acc_ref[CHUNK:, :] = jnp.zeros((CHUNK * (SLOTS - 1), WIDTH), F32)

    for k in range(CHUNKS):
        @pl.when(k < own_count)
        def _(k=k):
            own_q(k).wait()

    sweep(own_base, own_count, me * BLOCK, BLOCK, given)
    gather_first("kv")

    dq_in.wait()
    tail_in.wait()

    def tail_step(t, _):
        first = t * 8
        scores, kv = [], []
        col = lax.broadcasted_iota(jnp.int32, (8, 256), 1)
        for u in range(8):
            r = first + u
            kv.append(pl.ds(pl.multiple_of(r * 256, 256), 256))
            q16 = qbuf[pl.ds(pl.multiple_of((first + u // 2 * 2) * 8, 16), 16), :]
            s = lax.dot_general(q16, tailbuf[kv[u], :], NT, preferred_element_type=F32)
            s = s[u % 2 * 8:u % 2 * 8 + 8]
            seen = jnp.logical_and(col % 2 == 0, col < 2 * len_ref[r])
            scores.append(jnp.where(seen, s, LOW_FILL))
        s = jnp.concatenate(scores, axis=0)
        m_new = jnp.broadcast_to(jnp.max(s, axis=1, keepdims=True), (64, WIDTH))
        p = jnp.exp2((s - wide(m_new, 256)) * SCALE)
        here = pl.ds(pl.multiple_of(t * 64, 64), 64)
        m_ref[here, :] = m_new
        l_ref[here, :] = p[:, :WIDTH] + p[:, WIDTH:]
        p = pltpu.roll(p, 1, 1).astype(BF16)
        out = []
        for u in range(8):
            p16 = p[u // 2 * 16:u // 2 * 16 + 16]
            o = jnp.dot(p16, tailbuf[kv[u], :], preferred_element_type=F32)
            out.append(o[u % 2 * 8:u % 2 * 8 + 8])
        acc_ref[here, :] = jnp.concatenate(out, axis=0)
        return 0

    lax.fori_loop(0, 8, tail_step, 0)

    arrived("kv", OWN, 1)
    decode_step(ctx)

    @pl.when(rep == 1)
    def _():
        sweep(own_base, own_count, (me - 1) * BLOCK, BLOCK)

    for k in range(GUESTS):
        @pl.when(k < guests)
        def _(k=k):
            guest_q(k).wait_recv()

    both_blocks(ctx)
    arrived("kv", XP, 1)
    decode_step(chips[XP])
    both_blocks(chips[XP])
    gather_second("kv")
    arrived("kv", ZM, 1)
    decode_step(chips[ZM])
    arrived("kv", ZP, 1)
    decode_step(chips[ZP])
    both_blocks(chips[ZM])
    gather_third("kv")
    for s in (ZMX, ZPX, ZZ, ZZX):
        arrived("kv", s, 1)
        decode_step(chips[s])

    total = jnp.sum(l_ref[:CHUNK, :], axis=1, keepdims=True)
    fbuf[...] = acc_ref[:CHUNK, :] / total
    mine = pl.ds(pl.multiple_of(me * 64, 64), 64)
    for h in range(8):
        att[mine, h * WIDTH:(h + 1) * WIDTH] = fbuf[pl.ds(h, 64, stride=8), :].astype(BF16)
    gather_start("att")

    both_blocks(chips[ZP])
    gather_first("att")
    both_blocks(chips[ZMX])
    gather_second("att")
    both_blocks(chips[ZPX])
    gather_third("att")

    w_in.wait()

    def rs_copy(chip, sem):
        return pltpu.make_async_remote_copy(
            src_ref=part.at[pl.ds(pl.multiple_of(chip * 128, 128), 128)],
            dst_ref=landed.at[pl.ds(pl.multiple_of(head * 128, 128), 128)],
            send_sem=rs_sem.at[0, sem], recv_sem=rs_sem.at[1, head],
            device_id={"head": chip}, device_id_type=MESH,
        )

    arrived("att", OWN, 1)
    for s in range(1, 8):
        arrived("att", s, 1)

    def project(k, _):
        chip = (head + k) % 8
        rows_here = pl.ds(pl.multiple_of(chip * 128, 128), 128)
        part[rows_here, :] = jnp.dot(
            att[rows_here, :], wbuf[...], preferred_element_type=F32
        ).astype(BF16)

        @pl.when(k > 0)
        def _():
            rs_copy(chip, k).start()

        return 0

    lax.fori_loop(0, 8, project, 0)

    both_blocks(chips[ZZ])
    both_blocks(chips[ZZX])

    @pl.when(guests > 0)
    def _():
        sweep(1, guests, mate * BLOCK, BLOCK, 0)

        @pl.when(mate % 2 == 1)
        def _():
            sweep(1, guests, (mate - 1) * BLOCK, BLOCK)

    def finish(slot):
        r = rows_of(slot)
        obuf[r, :] = (
            acc_ref[r, :] / jnp.sum(l_ref[r, :], axis=1, keepdims=True)
        ).astype(BF16)

    def give_back(k):
        return pltpu.make_async_remote_copy(
            src_ref=obuf.at[pl.ds((1 + k) * CHUNK, CHUNK)],
            dst_ref=out_hbm.at[pl.ds(k * CHUNK, CHUNK)],
            send_sem=back_sem.at[0, k], recv_sem=back_sem.at[1, k],
            device_id=to_mate, device_id_type=MESH,
        )

    for k in range(GUESTS):
        @pl.when(k < guests)
        def _(k=k):
            finish(1 + k)
            give_back(k).start()

    def own_out(k):
        return pltpu.make_async_copy(
            obuf.at[pl.ds(pl.multiple_of((own_base + k) * CHUNK, CHUNK), CHUNK)],
            out_hbm.at[pl.ds(pl.multiple_of((given + k) * CHUNK, CHUNK), CHUNK)],
            out_sem.at[k],
        )

    for k in range(CHUNKS):
        @pl.when(k < own_count)
        def _(k=k):
            finish(own_base + k)
            own_out(k).start()

    mine = pl.ds(pl.multiple_of(head * 128, 128), 128)
    total = part[mine, :].astype(F32)
    for away in range(1, 8):
        other = (head + away) % 8
        there = landed.at[pl.ds(pl.multiple_of(other * 128, 128), 128)]
        pltpu.make_async_remote_copy(
            src_ref=there, dst_ref=there, send_sem=rs_sem.at[0, 0],
            recv_sem=rs_sem.at[1, other], device_id={"head": other}, device_id_type=MESH,
        ).wait_recv()
        total = total + landed[pl.ds(pl.multiple_of(other * 128, 128), 128), :].astype(F32)
    dec_ref[...] = total.astype(BF16)

    for copy in sends:
        copy.wait_send()
    for k in range(1, 8):
        rs_copy((head + k) % 8, k).wait_send()
    for k in range(GUESTS):
        @pl.when(k < given)
        def _(k=k):
            guest_q(k).wait_send()
            give_back(k).wait_recv()

        @pl.when(k < guests)
        def _(k=k):
            give_back(k).wait_send()
    for k in range(CHUNKS):
        @pl.when(k < own_count)
        def _(k=k):
            own_out(k).wait()


def on_device(prefix_query, prefix_kv, decode_query, tail_key_value, tail_len, out_weight):
    any_space = pl.BlockSpec(memory_space=pl.ANY)
    prefix_out, decoded = pl.pallas_call(
        kernel,
        out_shape=(
            jax.ShapeDtypeStruct((CHUNKS * CHUNK, WIDTH), BF16),
            jax.ShapeDtypeStruct((128, 512), BF16),
        ),
        in_specs=[any_space] * 4 + [pl.BlockSpec(memory_space=pltpu.SMEM), any_space],
        out_specs=(any_space, pl.BlockSpec(memory_space=pltpu.VMEM)),
        scratch_shapes=[
            pltpu.VMEM((2 * BLOCK, WIDTH), BF16),
            pltpu.VMEM((16 * BLOCK, WIDTH), BF16),
            pltpu.VMEM((16 * BLOCK, WIDTH), BF16),
            pltpu.VMEM((SLOTS * CHUNK, WIDTH), BF16),
            pltpu.VMEM((64 * 256, WIDTH), BF16),
            pltpu.VMEM((1024, 512), BF16),
            pltpu.VMEM((SLOTS * CHUNK, WIDTH), F32),
            pltpu.VMEM((SLOTS * CHUNK, WIDTH), F32),
            pltpu.VMEM((SLOTS * CHUNK, WIDTH), F32),
            pltpu.VMEM((SLOTS * CHUNK, WIDTH), BF16),
            pltpu.VMEM((CHUNK, WIDTH), F32),
            pltpu.VMEM((1024, 1024), BF16),
            pltpu.VMEM((1024, 512), BF16),
            pltpu.VMEM((1024, 512), BF16),
            pltpu.SemaphoreType.DMA((4,)),
            pltpu.SemaphoreType.DMA((CHUNKS,)),
            pltpu.SemaphoreType.DMA((64,)),
            pltpu.SemaphoreType.DMA((8, 2, 2)),
            pltpu.SemaphoreType.DMA((8, 2, 2)),
            pltpu.SemaphoreType.DMA((2, GUESTS)),
            pltpu.SemaphoreType.DMA((2, GUESTS)),
            pltpu.SemaphoreType.DMA((2, 8)),
            pltpu.SemaphoreType.DMA((CHUNKS,)),
        ],
        compiler_params=pltpu.CompilerParams(
            collective_id=0, has_side_effects=True, vmem_limit_bytes=56 << 20
        ),
        name="layer_attention",
    )(
        prefix_query.reshape(CHUNKS * CHUNK, WIDTH),
        prefix_kv.reshape(2 * BLOCK, WIDTH),
        decode_query.reshape(CHUNK, WIDTH),
        tail_key_value.reshape(64 * 256, WIDTH),
        tail_len,
        out_weight,
    )
    return prefix_out.reshape(prefix_query.shape), decoded


def solution(mesh):
    return jax.shard_map(
        on_device,
        mesh=mesh,
        in_specs=(
            P(("ctx", "rep"), "head", None),
            P(("ctx", "rep"), "head", None, None),
            P(("ctx", "rep"), "head", None),
            P(("ctx", "rep"), None, "head", None, None),
            P(("ctx", "rep")),
            P("head", ("ctx", "rep")),
        ),
        out_specs=(P(("ctx", "rep"), "head", None), P("head", ("ctx", "rep"))),
        check_vma=False,
    )
```

```python
import functools

import jax
import jax.numpy as jnp
from jax import lax
from jax.experimental import pallas as pl
from jax.experimental.pallas import tpu as pltpu
from jax.sharding import PartitionSpec as P

F32, BF16 = jnp.float32, jnp.bfloat16
MESH = pl.DeviceIdType.MESH
LOW_FILL = -1e30
WIDTH = 128
SCALE = WIDTH**-0.5 * 1.4426950408889634
BLOCK = 512
CHUNK = 512
CHUNKS = 8
GUESTS = 4
GUEST_BASE = 1 + CHUNKS
SLOTS = 1 + CHUNKS + GUESTS + 1
NT = (((1,), (1,)), ((), ()))
EARLY = 1
ROLLS = 16
ITEMS = (3, 4)


def wide(column, width):
    return jnp.concatenate([column] * (width // WIDTH), axis=1)


def kernel(
    q_hbm, kv_hbm, dq_hbm, tail_hbm, len_ref, w_hbm,
    out_hbm, landed,
    kvint, kbuf, vbuf, qbuf, tailbuf, wbuf, m_ref, l_ref, acc_ref,
    obuf, fbuf, ahead, att, part,
    in_sem, q_sem, send_sem, kv_sem, att_sem, guest_sem, back_sem, rs_sem, out_sem,
):
    ctx, head, rep = lax.axis_index("ctx"), lax.axis_index("head"), lax.axis_index("rep")
    z, x = ctx // 2, ctx % 2
    me = ctx * 2 + rep
    mate = 15 - me
    late = me >= 8
    def shared(i):
        return i // 2 - 3 - jnp.where(i == 8, 1, 0)

    guests = jnp.where(late, 0, shared(mate))
    given = jnp.where(late, shared(me), 0)
    own_base = 1
    own_count = CHUNKS - given

    def place(dz, flip):
        return ((z + dz) % 4) * 2 + (1 - x if flip else x)

    chips = [ctx, place(0, True), place(1, False), place(3, False),
             place(1, True), place(3, True), place(2, False), place(2, True)]
    OWN, XP, ZP, ZM, ZPX, ZMX, ZZ, ZZX = range(8)

    sibling = {"ctx": ctx, "rep": 1 - rep}
    over_x = {"ctx": chips[XP], "rep": rep}
    over_zp = {"ctx": chips[ZP], "rep": rep}
    over_zm = {"ctx": chips[ZM], "rep": rep}
    to_mate = {"ctx": mate // 2, "rep": mate % 2}

    def load(src, dst, sem):
        copy = pltpu.make_async_copy(src, dst, sem)
        copy.start()
        return copy

    kv_in = load(kv_hbm, kvint, in_sem.at[0])
    dq_in = load(dq_hbm, qbuf.at[pl.ds(0, CHUNK)], in_sem.at[1])

    def own_q(k):
        return pltpu.make_async_copy(
            q_hbm.at[pl.ds(pl.multiple_of((given + k) * CHUNK, CHUNK), CHUNK)],
            qbuf.at[pl.ds(pl.multiple_of((own_base + k) * CHUNK, CHUNK), CHUNK)],
            q_sem.at[k],
        )

    for k in range(CHUNKS):
        @pl.when(k < own_count)
        def _(k=k):
            own_q(k).start()

    m_ref[...] = jnp.full(m_ref.shape, LOW_FILL, F32)
    l_ref[...] = jnp.zeros(l_ref.shape, F32)
    acc_ref[...] = jnp.zeros(acc_ref.shape, F32)

    tail_in = load(tail_hbm, tailbuf, in_sem.at[2])
    w_in = load(w_hbm, wbuf, in_sem.at[3])

    barrier = pltpu.get_barrier_semaphore()
    for device in (sibling, over_x, over_zp, over_zm, to_mate):
        pl.semaphore_signal(barrier, inc=1, device_id=device, device_id_type=MESH)
    for away in range(1, 8):
        pl.semaphore_signal(
            barrier, inc=1, device_id={"head": (head + away) % 8}, device_id_type=MESH
        )

    rows = lax.broadcasted_iota(jnp.int32, (256, 256), 0)
    cols = lax.broadcasted_iota(jnp.int32, (256, 256), 1)
    wanted = jnp.where(rows < 128, rows * 2, (rows - 128) * 2 + 1)
    pick = jnp.where(cols == wanted, 1.0, 0.0).astype(BF16)
    kv_in.wait()
    for t in range(4):
        apart = jnp.dot(pick, kvint[t * 256:(t + 1) * 256, :], preferred_element_type=F32)
        apart = apart.astype(BF16)
        here = pl.ds(pl.multiple_of(me * BLOCK + t * 128, 128), 128)
        kbuf[here, :] = apart[:128]
        vbuf[here, :] = apart[128:]

    pl.semaphore_wait(barrier, 12)

    sends = []

    def block_of(which, s, kind, piece):
        b = chips[s] * 2 + (rep if kind == 0 else 1 - rep)
        if which == "kv":
            ref = kbuf if piece == 0 else vbuf
            return ref.at[pl.ds(pl.multiple_of(b * BLOCK, BLOCK), BLOCK)]
        return att.at[pl.ds(pl.multiple_of(b * 64 + piece * 32, 32), 32)]

    def sem_of(which):
        return kv_sem if which == "kv" else att_sem

    def send(which, s, piece, device, s_there, kind_there):
        arguments = (which, s, piece, device, s_there, kind_there, len(sends))
        sends.append(arguments)
        sent(*arguments).start()

    def sent(which, s, piece, device, s_there, kind_there, number):
        return pltpu.make_async_remote_copy(
            src_ref=block_of(which, s, 0, piece),
            dst_ref=block_of(which, s, 0, piece),
            send_sem=send_sem.at[number],
            recv_sem=sem_of(which).at[s_there, kind_there, piece],
            device_id=device,
            device_id_type=MESH,
        )

    def arrived(which, s, kind, pieces=(0, 1)):
        for piece in pieces:
            ref = block_of(which, s, kind, piece)
            pltpu.make_async_remote_copy(
                src_ref=ref, dst_ref=ref, send_sem=send_sem.at[0],
                recv_sem=sem_of(which).at[s, kind, piece],
                device_id=sibling, device_id_type=MESH,
            ).wait_recv()

    def both(which, s, device, s_there, kind_there):
        for piece in (0, 1):
            send(which, s, piece, device, s_there, kind_there)

    def gather_start(which):
        both(which, OWN, over_zp, ZM, 0)
        both(which, OWN, over_zm, ZP, 0)
        both(which, OWN, over_x, XP, 0)
        both(which, OWN, sibling, OWN, 1)

    def gather_first(which):
        arrived(which, ZM, 0)
        send(which, ZM, 0, over_zp, ZZ, 0)
        arrived(which, ZP, 0)
        send(which, ZP, 1, over_zm, ZZ, 0)
        arrived(which, XP, 0)
        both(which, XP, over_zp, ZMX, 0)
        both(which, XP, over_zm, ZPX, 0)
        for s in (XP, ZM, ZP):
            both(which, s, sibling, s, 1)

    def gather_second(which):
        arrived(which, ZZ, 0)
        both(which, ZZ, over_x, ZZX, 0)
        both(which, ZZ, sibling, ZZ, 1)

    def gather_third(which):
        for s in (ZMX, ZPX, ZZX):
            arrived(which, s, 0)
            both(which, s, sibling, s, 1)

    gather_start("kv")

    def guest_q(k):
        return pltpu.make_async_remote_copy(
            src_ref=q_hbm.at[pl.ds(pl.multiple_of(k * CHUNK, CHUNK), CHUNK)],
            dst_ref=qbuf.at[pl.ds(pl.multiple_of((GUEST_BASE + k) * CHUNK, CHUNK), CHUNK)],
            send_sem=guest_sem.at[0, k], recv_sem=guest_sem.at[1, k],
            device_id=to_mate, device_id_type=MESH,
        )

    def rows_of(slot):
        return pl.ds(pl.multiple_of(slot * CHUNK, CHUNK), CHUNK)

    def absorb(slots, ranges, seen=None):
        where = [rows_of(slot) for slot in slots]
        keys = [pl.ds(pl.multiple_of(first, BLOCK), count) for first, count in ranges]
        old = [(m_ref[r, :], l_ref[r, :], acc_ref[r, :]) for r in where]
        scores = [
            [lax.dot_general(qbuf[r, :], kbuf[k, :], NT, preferred_element_type=F32) for k in keys]
            for r in where
        ]
        result = []
        for i, (m_old, l_old, a_old) in enumerate(old):
            parts = scores[i]
            if seen is not None:
                parts = [
                    jnp.concatenate(
                        [
                            jnp.where(
                                ahead[...] <= seen[i] - j * WIDTH,
                                s[:, j * WIDTH:(j + 1) * WIDTH],
                                LOW_FILL,
                            )
                            for j in range(s.shape[1] // WIDTH)
                        ],
                        axis=1,
                    )
                    for s in parts
                ]
            m_new = functools.reduce(
                jnp.maximum, [jnp.max(s, axis=1, keepdims=True) for s in parts], m_old
            )
            factor = jnp.exp2((m_old - m_new) * SCALE)
            total, mixed = l_old * factor, a_old * factor
            for s, k in zip(parts, keys):
                p = jnp.exp2((s - wide(m_new, s.shape[1])) * SCALE)
                for j in range(s.shape[1] // WIDTH):
                    total = total + p[:, j * WIDTH:(j + 1) * WIDTH]
                mixed = mixed + jnp.dot(p.astype(BF16), vbuf[k, :], preferred_element_type=F32)
            result.append((m_new, total, mixed))
        for i, r in enumerate(where):
            m_ref[r, :], l_ref[r, :], acc_ref[r, :] = result[i]

    def first_items(slot, pairs, who, place):
        blocks = who % 2 + 1

        def step(t, _):
            pair, b = t // blocks, t % blocks
            last = b == blocks - 1
            seen = [
                jnp.where(last, (place + 2 * pair + i) * 64, 2 * BLOCK) for i in range(2)
            ]
            absorb(
                [slot + 2 * pair, slot + 2 * pair + 1],
                [((who - blocks + 1 + b) * BLOCK, BLOCK)],
                seen,
            )
            return 0

        lax.fori_loop(0, pairs * blocks, step, 0)

    def half_items(slot, count, who):
        def step(k, _):
            absorb([slot + k], [(who // 4 * 4 * BLOCK, 2 * BLOCK)])
            return 0

        lax.fori_loop(0, jnp.where(who // 2 % 2 == 1, count, 0), step, 0)

    def pick_chip(k, group):
        return functools.reduce(
            lambda rest, n: jnp.where(k == n, chips[group[n]], rest),
            range(1, len(group)),
            chips[group[0]],
        )

    def decode_items(first, second):
        def step(k, _):
            where = (pick_chip(k, first), pick_chip(k, second))
            absorb([0], [(chip * 2 * BLOCK, 2 * BLOCK) for chip in where])
            return 0

        lax.fori_loop(0, 2, step, 0)

    def finish(slot):
        r = rows_of(slot)
        obuf[r, :] = (
            acc_ref[r, :] / jnp.sum(l_ref[r, :], axis=1, keepdims=True)
        ).astype(BF16)

    def own_out(k):
        return pltpu.make_async_copy(
            obuf.at[pl.ds(pl.multiple_of((own_base + k) * CHUNK, CHUNK), CHUNK)],
            out_hbm.at[pl.ds(pl.multiple_of((given + k) * CHUNK, CHUNK), CHUNK)],
            out_sem.at[k],
        )

    def give(lo, hi):
        for k in range(lo, hi):
            @pl.when(k < given)
            def _(k=k):
                guest_q(k).start()

    ahead[...] = (
        lax.broadcasted_iota(jnp.int32, (CHUNK, WIDTH), 1)
        - lax.broadcasted_iota(jnp.int32, (CHUNK, WIDTH), 0) // 8
    )

    dq_in.wait()
    tail_in.wait()

    def tail_step(t, _):
        first = t * ROLLS
        scores, kv = [], []
        col = lax.broadcasted_iota(jnp.int32, (8, 256), 1)
        even = jnp.where(col % 2 == 0, col, 512)
        for u in range(ROLLS):
            r = first + u
            kv.append(pl.ds(pl.multiple_of(r * 256, 256), 256))
            q16 = qbuf[pl.ds(pl.multiple_of((first + u // 2 * 2) * 8, 16), 16), :]
            s = lax.dot_general(q16, tailbuf[kv[u], :], NT, preferred_element_type=F32)
            s = s[u % 2 * 8:u % 2 * 8 + 8]
            scores.append(jnp.where(even < 2 * len_ref[r], s, LOW_FILL))
        s = jnp.concatenate(scores, axis=0)
        m_new = jnp.broadcast_to(jnp.max(s, axis=1, keepdims=True), (8 * ROLLS, WIDTH))
        p = jnp.exp2((s - wide(m_new, 256)) * SCALE)
        here = pl.ds(pl.multiple_of(t * 8 * ROLLS, 8 * ROLLS), 8 * ROLLS)
        m_ref[here, :] = m_new
        l_ref[here, :] = p[:, :WIDTH] + p[:, WIDTH:]
        p = pltpu.roll(p, 1, 1).astype(BF16)
        out = []
        for u in range(ROLLS):
            p16 = p[u // 2 * 16:u // 2 * 16 + 16]
            o = jnp.dot(p16, tailbuf[kv[u], :], preferred_element_type=F32)
            out.append(o[u % 2 * 8:u % 2 * 8 + 8])
        acc_ref[here, :] = jnp.concatenate(out, axis=0)
        return 0

    lax.fori_loop(0, 64 // ROLLS, tail_step, 0)

    gather_first("kv")
    arrived("kv", OWN, 1)
    for k in range(CHUNKS):
        @pl.when(k < own_count)
        def _(k=k):
            own_q(k).wait()

    own_pairs = (own_count + 1) // 2
    first_items(own_base, own_pairs, me, given)
    gather_second("kv")
    give(0, EARLY)
    for s in (XP, ZM, ZP):
        arrived("kv", s, 1)
    decode_items((OWN, ZM), (XP, ZP))
    gather_third("kv")
    give(EARLY, GUESTS)
    for s in (ZZ, ZMX, ZPX, ZZX):
        arrived("kv", s, 1)
    decode_items((ZZ, ZPX), (ZMX, ZZX))

    total = jnp.sum(l_ref[:CHUNK, :], axis=1, keepdims=True)
    fbuf[...] = acc_ref[:CHUNK, :] / total
    mine = pl.ds(pl.multiple_of(me * 64, 64), 64)
    for h in range(8):
        att[mine, h * WIDTH:(h + 1) * WIDTH] = fbuf[pl.ds(h, 64, stride=8), :].astype(BF16)
    gather_start("att")

    def rs_copy(chip, number):
        return pltpu.make_async_remote_copy(
            src_ref=part.at[pl.ds(pl.multiple_of(chip * 128, 128), 128)],
            dst_ref=landed.at[pl.ds(pl.multiple_of(head * 128, 128), 128)],
            send_sem=rs_sem.at[0, number], recv_sem=rs_sem.at[1, head],
            device_id={"head": chip}, device_id_type=MESH,
        )

    def project(chip):
        rows_here = pl.ds(pl.multiple_of(chip * 128, 128), 128)
        part[rows_here, :] = jnp.dot(
            att[rows_here, :], wbuf[...], preferred_element_type=F32
        ).astype(BF16)

        @pl.when(chip != head)
        def _():
            rs_copy(chip, chip).start()

    def give_back(k):
        return pltpu.make_async_remote_copy(
            src_ref=obuf.at[pl.ds(pl.multiple_of((GUEST_BASE + k) * CHUNK, CHUNK), CHUNK)],
            dst_ref=out_hbm.at[pl.ds(pl.multiple_of(k * CHUNK, CHUNK), CHUNK)],
            send_sem=back_sem.at[0, k], recv_sem=back_sem.at[1, k],
            device_id=to_mate, device_id_type=MESH,
        )

    def projects(group):
        def step(k, _):
            project(pick_chip(k, group))
            return 0

        lax.fori_loop(0, len(group), step, 0)

    guest_planes = mate // 4
    guest_items = guests * guest_planes
    items = guest_items + own_count * z

    def plane_items(lo, hi):
        def step(t, _):
            foreign = t < guest_items
            after = jnp.where(foreign, t, t - guest_items)
            planes = jnp.maximum(jnp.where(foreign, guest_planes, z), 1)
            k, j = after // planes, after % planes
            slot = jnp.where(foreign, GUEST_BASE, own_base) + k
            absorb([slot], [(j * 4 * BLOCK, 4 * BLOCK)])

            @pl.when(j == planes - 1)
            def _():
                finish(slot)

                @pl.when(foreign)
                def _():
                    give_back(k).start()

                @pl.when(jnp.logical_not(foreign))
                def _():
                    own_out(k).start()

            return 0

        lax.fori_loop(lo, jnp.minimum(hi, items), step, 0)

    half_items(own_base, own_count, me)

    @pl.when(z == 0)
    def _():
        def step(k, _):
            finish(own_base + k)
            own_out(k).start()
            return 0

        lax.fori_loop(0, own_count, step, 0)

    gather_first("att")

    def guest_in(k, _):
        guest_q(k).wait_recv()
        return 0

    lax.fori_loop(0, guests, guest_in, 0)
    first_items(GUEST_BASE, (guests + 1) // 2, mate, 0)
    gather_second("att")
    half_items(GUEST_BASE, guests, mate)
    w_in.wait()
    for s in (OWN, XP, ZM, ZP):
        arrived("att", s, 1)
    projects((OWN, XP, ZM, ZP))
    plane_items(0, ITEMS[0])
    gather_third("att")
    plane_items(ITEMS[0], ITEMS[1])
    for s in (ZZ, ZMX, ZPX, ZZX):
        arrived("att", s, 1)
    projects((ZZ, ZMX, ZPX, ZZX))
    plane_items(ITEMS[1], 1000)

    own_part = pltpu.make_async_copy(
        part.at[pl.ds(pl.multiple_of(head * 128, 128), 128)],
        landed.at[pl.ds(pl.multiple_of(head * 128, 128), 128)],
        in_sem.at[0],
    )
    own_part.start()
    own_part.wait()
    for away in range(1, 8):
        other = (head + away) % 8
        there = landed.at[pl.ds(pl.multiple_of(other * 128, 128), 128)]
        pltpu.make_async_remote_copy(
            src_ref=there, dst_ref=there, send_sem=rs_sem.at[0, 0],
            recv_sem=rs_sem.at[1, other], device_id={"head": other}, device_id_type=MESH,
        ).wait_recv()

    for arguments in sends:
        sent(*arguments).wait_send()
    for k in range(1, 8):
        rs_copy((head + k) % 8, (head + k) % 8).wait_send()
    for k in range(GUESTS):
        @pl.when(k < given)
        def _(k=k):
            guest_q(k).wait_send()
            give_back(k).wait_recv()

        @pl.when(k < guests)
        def _(k=k):
            give_back(k).wait_send()
    for k in range(CHUNKS):
        @pl.when(k < own_count)
        def _(k=k):
            own_out(k).wait()


def last_kernel(rows_hbm, parts_hbm, out_hbm, dec_ref, parts, row_sem, part_sem):
    copies = []
    for k in range(8):
        here = pl.ds(k * 128, 128)
        copies.append(pltpu.make_async_copy(parts_hbm.at[here], parts.at[here], part_sem.at[k]))
    for k in range(8):
        here = pl.ds(k * CHUNK, CHUNK)
        copies.append(pltpu.make_async_copy(rows_hbm.at[here], out_hbm.at[here], row_sem.at[k]))
    for copy in copies:
        copy.start()
    total = jnp.zeros((128, 512), F32)
    for k in range(8):
        copies[k].wait()
        total = total + parts[k * 128:(k + 1) * 128, :].astype(F32)
    dec_ref[...] = total.astype(BF16)
    for copy in copies[8:]:
        copy.wait()


def on_device(prefix_query, prefix_kv, decode_query, tail_key_value, tail_len, out_weight):
    any_space = pl.BlockSpec(memory_space=pl.ANY)
    rows_out, parts = pl.pallas_call(
        kernel,
        out_shape=(
            jax.ShapeDtypeStruct((CHUNKS * CHUNK, WIDTH), BF16),
            jax.ShapeDtypeStruct((1024, 512), BF16),
        ),
        in_specs=[any_space] * 4 + [pl.BlockSpec(memory_space=pltpu.SMEM), any_space],
        out_specs=(any_space, any_space),
        scratch_shapes=[
            pltpu.VMEM((2 * BLOCK, WIDTH), BF16),
            pltpu.VMEM((16 * BLOCK, WIDTH), BF16),
            pltpu.VMEM((16 * BLOCK, WIDTH), BF16),
            pltpu.VMEM((SLOTS * CHUNK, WIDTH), BF16),
            pltpu.VMEM((64 * 256, WIDTH), BF16),
            pltpu.VMEM((1024, 512), BF16),
            pltpu.VMEM((SLOTS * CHUNK, WIDTH), F32),
            pltpu.VMEM((SLOTS * CHUNK, WIDTH), F32),
            pltpu.VMEM((SLOTS * CHUNK, WIDTH), F32),
            pltpu.VMEM((SLOTS * CHUNK, WIDTH), BF16),
            pltpu.VMEM((CHUNK, WIDTH), F32),
            pltpu.VMEM((CHUNK, WIDTH), jnp.int32),
            pltpu.VMEM((1024, 1024), BF16),
            pltpu.VMEM((1024, 512), BF16),
            pltpu.SemaphoreType.DMA((4,)),
            pltpu.SemaphoreType.DMA((CHUNKS,)),
            pltpu.SemaphoreType.DMA((64,)),
            pltpu.SemaphoreType.DMA((8, 2, 2)),
            pltpu.SemaphoreType.DMA((8, 2, 2)),
            pltpu.SemaphoreType.DMA((2, GUESTS)),
            pltpu.SemaphoreType.DMA((2, GUESTS)),
            pltpu.SemaphoreType.DMA((2, 8)),
            pltpu.SemaphoreType.DMA((CHUNKS,)),
        ],
        compiler_params=pltpu.CompilerParams(
            collective_id=0, has_side_effects=True, vmem_limit_bytes=56 << 20
        ),
        name="layer_attention",
    )(
        prefix_query.reshape(CHUNKS * CHUNK, WIDTH),
        prefix_kv.reshape(2 * BLOCK, WIDTH),
        decode_query.reshape(CHUNK, WIDTH),
        tail_key_value.reshape(64 * 256, WIDTH),
        tail_len,
        out_weight,
    )
    prefix_out, decoded = pl.pallas_call(
        last_kernel,
        out_shape=(
            jax.ShapeDtypeStruct((CHUNKS * CHUNK, WIDTH), BF16),
            jax.ShapeDtypeStruct((128, 512), BF16),
        ),
        in_specs=[any_space] * 2,
        out_specs=(any_space, pl.BlockSpec(memory_space=pltpu.VMEM)),
        scratch_shapes=[
            pltpu.VMEM((1024, 512), BF16),
            pltpu.SemaphoreType.DMA((8,)),
            pltpu.SemaphoreType.DMA((8,)),
        ],
        compiler_params=pltpu.CompilerParams(vmem_limit_bytes=8 << 20),
        name="results",
    )(rows_out, parts)
    return prefix_out.reshape(prefix_query.shape), decoded


def solution(mesh):
    return jax.shard_map(
        on_device,
        mesh=mesh,
        in_specs=(
            P(("ctx", "rep"), "head", None),
            P(("ctx", "rep"), "head", None, None),
            P(("ctx", "rep"), "head", None),
            P(("ctx", "rep"), None, "head", None, None),
            P(("ctx", "rep")),
            P("head", ("ctx", "rep")),
        ),
        out_specs=(P(("ctx", "rep"), "head", None), P("head", ("ctx", "rep"))),
        check_vma=False,
    )
```

```python
import functools

import jax
import jax.numpy as jnp
from jax import lax
from jax.experimental import pallas as pl
from jax.experimental.pallas import tpu as pltpu
from jax.sharding import PartitionSpec as P

F32, BF16 = jnp.float32, jnp.bfloat16
MESH = pl.DeviceIdType.MESH
LOW_FILL = -1e30
WIDTH = 128
SCALE = WIDTH**-0.5 * 1.4426950408889634
BLOCK = 512
CHUNK = 512
CHUNKS = 8
GUESTS = 4
GUEST_BASE = 1 + CHUNKS
SLOTS = 1 + CHUNKS + GUESTS + 1
NT = (((1,), (1,)), ((), ()))
EARLY = 1
ROLLS = 16
CHIP_ITEMS = (1, 2, 2, 1, 1)
PLANE_ITEMS = (1, 3)


def wide(column, width):
    return jnp.concatenate([column] * (width // WIDTH), axis=1)


def kernel(
    q_hbm, kv_hbm, dq_hbm, tail_hbm, len_ref, w_hbm,
    out_hbm, landed,
    kvint, kbuf, vbuf, qbuf, tailbuf, wbuf, m_ref, l_ref, acc_ref,
    obuf, fbuf, ahead, att, part,
    in_sem, q_sem, send_sem, kv_sem, att_sem, guest_sem, back_sem, rs_sem, out_sem,
):
    ctx, head, rep = lax.axis_index("ctx"), lax.axis_index("head"), lax.axis_index("rep")
    z, x = ctx // 2, ctx % 2
    me = ctx * 2 + rep
    mate = 15 - me
    late = me >= 8
    def shared(i):
        return (i - 7) * 7 // 16

    guests = jnp.where(late, 0, shared(mate))
    given = jnp.where(late, shared(me), 0)
    own_base = 1
    own_count = CHUNKS - given

    def place(dz, flip):
        return ((z + dz) % 4) * 2 + (1 - x if flip else x)

    chips = [ctx, place(0, True), place(1, False), place(3, False),
             place(1, True), place(3, True), place(2, False), place(2, True)]
    OWN, XP, ZP, ZM, ZPX, ZMX, ZZ, ZZX = range(8)

    sibling = {"ctx": ctx, "rep": 1 - rep}
    over_x = {"ctx": chips[XP], "rep": rep}
    over_zp = {"ctx": chips[ZP], "rep": rep}
    over_zm = {"ctx": chips[ZM], "rep": rep}
    to_mate = {"ctx": mate // 2, "rep": mate % 2}

    barrier = pltpu.get_barrier_semaphore()
    for device in (sibling, over_x, over_zp, over_zm, to_mate):
        pl.semaphore_signal(barrier, inc=1, device_id=device, device_id_type=MESH)
    for away in range(1, 8):
        pl.semaphore_signal(
            barrier, inc=1, device_id={"head": (head + away) % 8}, device_id_type=MESH
        )

    def load(src, dst, sem):
        copy = pltpu.make_async_copy(src, dst, sem)
        copy.start()
        return copy

    kv_in = load(kv_hbm, kvint, in_sem.at[0])
    dq_in = load(dq_hbm, qbuf.at[pl.ds(0, CHUNK)], in_sem.at[1])

    def own_q(k):
        return pltpu.make_async_copy(
            q_hbm.at[pl.ds(pl.multiple_of((given + k) * CHUNK, CHUNK), CHUNK)],
            qbuf.at[pl.ds(pl.multiple_of((own_base + k) * CHUNK, CHUNK), CHUNK)],
            q_sem.at[k],
        )

    for k in range(CHUNKS):
        @pl.when(k < own_count)
        def _(k=k):
            own_q(k).start()

    tail_in = load(tail_hbm, tailbuf, in_sem.at[2])
    w_in = load(w_hbm, wbuf, in_sem.at[3])

    rows = lax.broadcasted_iota(jnp.int32, (256, 256), 0)
    cols = lax.broadcasted_iota(jnp.int32, (256, 256), 1)
    wanted = jnp.where(rows < 128, rows * 2, (rows - 128) * 2 + 1)
    pick = jnp.where(cols == wanted, 1.0, 0.0).astype(BF16)
    kv_in.wait()
    for t in range(4):
        apart = jnp.dot(pick, kvint[t * 256:(t + 1) * 256, :], preferred_element_type=F32)
        apart = apart.astype(BF16)
        here = pl.ds(pl.multiple_of(me * BLOCK + t * 128, 128), 128)
        kbuf[here, :] = apart[:128]
        vbuf[here, :] = apart[128:]

    m_ref[...] = jnp.full(m_ref.shape, LOW_FILL, F32)
    l_ref[...] = jnp.zeros(l_ref.shape, F32)
    acc_ref[...] = jnp.zeros(acc_ref.shape, F32)
    ahead[...] = (
        lax.broadcasted_iota(jnp.int32, (CHUNK, WIDTH), 1)
        - lax.broadcasted_iota(jnp.int32, (CHUNK, WIDTH), 0) // 8
    )
    pl.semaphore_wait(barrier, 12)

    sends = []

    def block_of(which, s, kind, piece):
        b = chips[s] * 2 + (rep if kind == 0 else 1 - rep)
        if which == "kv":
            ref = kbuf if piece == 0 else vbuf
            return ref.at[pl.ds(pl.multiple_of(b * BLOCK, BLOCK), BLOCK)]
        return att.at[pl.ds(pl.multiple_of(b * 64 + piece * 32, 32), 32)]

    def sem_of(which):
        return kv_sem if which == "kv" else att_sem

    def send(which, s, piece, device, s_there, kind_there):
        arguments = (which, s, piece, device, s_there, kind_there, len(sends))
        sends.append(arguments)
        sent(*arguments).start()

    def sent(which, s, piece, device, s_there, kind_there, number):
        return pltpu.make_async_remote_copy(
            src_ref=block_of(which, s, 0, piece),
            dst_ref=block_of(which, s, 0, piece),
            send_sem=send_sem.at[number],
            recv_sem=sem_of(which).at[s_there, kind_there, piece],
            device_id=device,
            device_id_type=MESH,
        )

    def arrived(which, s, kind, pieces=(0, 1)):
        for piece in pieces:
            ref = block_of(which, s, kind, piece)
            pltpu.make_async_remote_copy(
                src_ref=ref, dst_ref=ref, send_sem=send_sem.at[0],
                recv_sem=sem_of(which).at[s, kind, piece],
                device_id=sibling, device_id_type=MESH,
            ).wait_recv()

    def both(which, s, device, s_there, kind_there):
        for piece in (0, 1):
            send(which, s, piece, device, s_there, kind_there)

    def gather_start(which):
        both(which, OWN, over_zp, ZM, 0)
        both(which, OWN, over_zm, ZP, 0)
        both(which, OWN, over_x, XP, 0)
        both(which, OWN, sibling, OWN, 1)

    def gather_first(which):
        arrived(which, ZM, 0)
        send(which, ZM, 0, over_zp, ZZ, 0)
        arrived(which, ZP, 0)
        send(which, ZP, 1, over_zm, ZZ, 0)
        arrived(which, XP, 0)
        both(which, XP, over_zp, ZMX, 0)
        both(which, XP, over_zm, ZPX, 0)
        for s in (XP, ZM, ZP):
            both(which, s, sibling, s, 1)

    def gather_second(which):
        arrived(which, ZZ, 0)
        both(which, ZZ, over_x, ZZX, 0)
        both(which, ZZ, sibling, ZZ, 1)

    def gather_third(which):
        for s in (ZMX, ZPX, ZZX):
            arrived(which, s, 0)
            both(which, s, sibling, s, 1)

    gather_start("kv")

    def guest_q(k):
        return pltpu.make_async_remote_copy(
            src_ref=q_hbm.at[pl.ds(pl.multiple_of(k * CHUNK, CHUNK), CHUNK)],
            dst_ref=qbuf.at[pl.ds(pl.multiple_of((GUEST_BASE + k) * CHUNK, CHUNK), CHUNK)],
            send_sem=guest_sem.at[0, k], recv_sem=guest_sem.at[1, k],
            device_id=to_mate, device_id_type=MESH,
        )

    def rows_of(slot):
        return pl.ds(pl.multiple_of(slot * CHUNK, CHUNK), CHUNK)

    def absorb(slots, ranges, seen=None):
        where = [rows_of(slot) for slot in slots]
        keys = [pl.ds(pl.multiple_of(first, BLOCK), count) for first, count in ranges]
        old = [(m_ref[r, :], l_ref[r, :], acc_ref[r, :]) for r in where]
        scores = [
            [lax.dot_general(qbuf[r, :], kbuf[k, :], NT, preferred_element_type=F32) for k in keys]
            for r in where
        ]
        result = []
        for i, (m_old, l_old, a_old) in enumerate(old):
            parts = scores[i]
            if seen is not None:
                parts = [
                    jnp.concatenate(
                        [
                            jnp.where(
                                ahead[...] <= seen[i] - j * WIDTH,
                                s[:, j * WIDTH:(j + 1) * WIDTH],
                                LOW_FILL,
                            )
                            for j in range(s.shape[1] // WIDTH)
                        ],
                        axis=1,
                    )
                    for s in parts
                ]
            m_new = functools.reduce(
                jnp.maximum, [jnp.max(s, axis=1, keepdims=True) for s in parts], m_old
            )
            factor = jnp.exp2((m_old - m_new) * SCALE)
            total, mixed = l_old * factor, a_old * factor
            for s, k in zip(parts, keys):
                p = jnp.exp2((s - wide(m_new, s.shape[1])) * SCALE)
                for j in range(s.shape[1] // WIDTH):
                    total = total + p[:, j * WIDTH:(j + 1) * WIDTH]
                mixed = mixed + jnp.dot(p.astype(BF16), vbuf[k, :], preferred_element_type=F32)
            result.append((m_new, total, mixed))
        for i, r in enumerate(where):
            m_ref[r, :], l_ref[r, :], acc_ref[r, :] = result[i]

    def first_items(slot, lo, hi, who, place):
        blocks = who % 2 + 1

        def step(t, _):
            pair, b = t // blocks, t % blocks
            last = b == blocks - 1
            seen = [
                jnp.where(last, (place + 2 * pair + i) * 64, 2 * BLOCK) for i in range(2)
            ]
            absorb(
                [slot + 2 * pair, slot + 2 * pair + 1],
                [((who - blocks + 1 + b) * BLOCK, BLOCK)],
                seen,
            )
            return 0

        lax.fori_loop(lo * blocks, hi * blocks, step, 0)

    def half_items(slot, lo, hi, who):
        def step(k, _):
            absorb([slot + k], [(who // 4 * 4 * BLOCK, 2 * BLOCK)])
            return 0

        lax.fori_loop(lo, jnp.where(who // 2 % 2 == 1, hi, lo), step, 0)

    before = jnp.where(z > 0, 1, 0)
    own_pairs = (own_count + 1) // 2
    chip_early = own_pairs * (x + before)
    chip_all = chip_early + own_pairs * before

    def chip_items(lo, hi):
        def step(t, _):
            b, k = t // own_pairs, t % own_pairs
            chip = jnp.where(
                jnp.logical_and(x == 1, b == 0),
                chips[XP],
                jnp.where(b == x, chips[ZM], chips[ZMX]),
            )
            absorb([own_base + 2 * k, own_base + 2 * k + 1], [(chip * 2 * BLOCK, 2 * BLOCK)])
            return 0

        lax.fori_loop(lo, hi, step, 0)

    def pick_chip(k, group):
        return functools.reduce(
            lambda rest, n: jnp.where(k == n, chips[group[n]], rest),
            range(1, len(group)),
            chips[group[0]],
        )

    def decode_items(first, second):
        def step(k, _):
            where = (pick_chip(k, first), pick_chip(k, second))
            absorb([0], [(chip * 2 * BLOCK, 2 * BLOCK) for chip in where])
            return 0

        lax.fori_loop(0, 2, step, 0)

    def finish(slot):
        r = rows_of(slot)
        obuf[r, :] = (
            acc_ref[r, :] / jnp.sum(l_ref[r, :], axis=1, keepdims=True)
        ).astype(BF16)

    def own_out(k):
        return pltpu.make_async_copy(
            obuf.at[pl.ds(pl.multiple_of((own_base + k) * CHUNK, CHUNK), CHUNK)],
            out_hbm.at[pl.ds(pl.multiple_of((given + k) * CHUNK, CHUNK), CHUNK)],
            out_sem.at[k],
        )

    def give(lo, hi):
        for k in range(lo, hi):
            @pl.when(k < given)
            def _(k=k):
                guest_q(k).start()

    dq_in.wait()
    tail_in.wait()

    def tail_step(t, _):
        first = t * ROLLS
        scores, kv = [], []
        col = lax.broadcasted_iota(jnp.int32, (8, 256), 1)
        even = jnp.where(col % 2 == 0, col, 512)
        for u in range(ROLLS):
            r = first + u
            kv.append(pl.ds(pl.multiple_of(r * 256, 256), 256))
            q16 = qbuf[pl.ds(pl.multiple_of((first + u // 2 * 2) * 8, 16), 16), :]
            s = lax.dot_general(q16, tailbuf[kv[u], :], NT, preferred_element_type=F32)
            s = s[u % 2 * 8:u % 2 * 8 + 8]
            scores.append(jnp.where(even < 2 * len_ref[r], s, LOW_FILL))
        s = jnp.concatenate(scores, axis=0)
        m_new = jnp.broadcast_to(jnp.max(s, axis=1, keepdims=True), (8 * ROLLS, WIDTH))
        p = jnp.exp2((s - wide(m_new, 256)) * SCALE)
        here = pl.ds(pl.multiple_of(t * 8 * ROLLS, 8 * ROLLS), 8 * ROLLS)
        m_ref[here, :] = m_new
        l_ref[here, :] = p[:, :WIDTH] + p[:, WIDTH:]
        p = pltpu.roll(p, 1, 1).astype(BF16)
        out = []
        for u in range(ROLLS):
            p16 = p[u // 2 * 16:u // 2 * 16 + 16]
            o = jnp.dot(p16, tailbuf[kv[u], :], preferred_element_type=F32)
            out.append(o[u % 2 * 8:u % 2 * 8 + 8])
        acc_ref[here, :] = jnp.concatenate(out, axis=0)
        return 0

    lax.fori_loop(0, 64 // ROLLS, tail_step, 0)

    arrived("kv", OWN, 1)
    for k in range(CHUNKS):
        @pl.when(k < own_count)
        def _(k=k):
            own_q(k).wait()

    first_items(own_base, 0, 2, me, given)
    gather_first("kv")
    first_items(own_base, 2, own_pairs, me, given)
    gather_second("kv")
    give(0, EARLY)
    for s in (XP, ZM, ZP):
        arrived("kv", s, 1)
    decode_items((OWN, ZM), (XP, ZP))
    chip_done = jnp.minimum(chip_early, CHIP_ITEMS[0])
    chip_items(0, chip_done)
    gather_third("kv")
    give(EARLY, GUESTS)
    for s in (ZZ, ZMX, ZPX, ZZX):
        arrived("kv", s, 1)
    decode_items((ZZ, ZPX), (ZMX, ZZX))

    total = jnp.sum(l_ref[:CHUNK, :], axis=1, keepdims=True)
    fbuf[...] = acc_ref[:CHUNK, :] / total
    mine = pl.ds(pl.multiple_of(me * 64, 64), 64)
    for h in range(8):
        att[mine, h * WIDTH:(h + 1) * WIDTH] = fbuf[pl.ds(h, 64, stride=8), :].astype(BF16)
    gather_start("att")

    def rs_copy(chip, number):
        return pltpu.make_async_remote_copy(
            src_ref=part.at[pl.ds(pl.multiple_of(chip * 128, 128), 128)],
            dst_ref=landed.at[pl.ds(pl.multiple_of(head * 128, 128), 128)],
            send_sem=rs_sem.at[0, number], recv_sem=rs_sem.at[1, head],
            device_id={"head": chip}, device_id_type=MESH,
        )

    def project(chip):
        rows_here = pl.ds(pl.multiple_of(chip * 128, 128), 128)
        part[rows_here, :] = jnp.dot(
            att[rows_here, :], wbuf[...], preferred_element_type=F32
        ).astype(BF16)

        @pl.when(chip != head)
        def _():
            rs_copy(chip, chip).start()

    def give_back(k):
        return pltpu.make_async_remote_copy(
            src_ref=obuf.at[pl.ds(pl.multiple_of((GUEST_BASE + k) * CHUNK, CHUNK), CHUNK)],
            dst_ref=out_hbm.at[pl.ds(pl.multiple_of(k * CHUNK, CHUNK), CHUNK)],
            send_sem=back_sem.at[0, k], recv_sem=back_sem.at[1, k],
            device_id=to_mate, device_id_type=MESH,
        )

    def projects(group):
        def step(k, _):
            project(pick_chip(k, group))
            return 0

        lax.fori_loop(0, len(group), step, 0)

    guest_planes, own_planes = mate // 4, jnp.maximum(z - 1, 0)
    guest_items = guests * guest_planes
    items = guest_items + own_count * own_planes

    def plane_items(lo, hi):
        def step(t, _):
            foreign = t < guest_items
            after = jnp.where(foreign, t, t - guest_items)
            planes = jnp.maximum(jnp.where(foreign, guest_planes, own_planes), 1)
            k, j = after // planes, after % planes
            slot = jnp.where(foreign, GUEST_BASE, own_base) + k
            absorb([slot], [(j * 4 * BLOCK, 4 * BLOCK)])

            @pl.when(j == planes - 1)
            def _():
                finish(slot)

                @pl.when(foreign)
                def _():
                    give_back(k).start()

                @pl.when(jnp.logical_not(foreign))
                def _():
                    own_out(k).start()

            return 0

        lax.fori_loop(lo, hi, step, 0)

    w_in.wait()
    chip_next = jnp.minimum(chip_done + CHIP_ITEMS[1], chip_all)
    chip_items(chip_done, chip_next)
    arrived("att", OWN, 1)
    project(ctx)
    gather_first("att")

    def guest_in(k, _):
        guest_q(k).wait_recv()
        return 0

    def guests_in(lo, hi):
        hi = jnp.minimum(hi, guests)
        lax.fori_loop(lo, hi, guest_in, 0)
        first_items(GUEST_BASE, lo // 2, (hi + 1) // 2, mate, 0)
        half_items(GUEST_BASE, lo, hi, mate)

    guests_in(0, 2)
    chip_last = jnp.minimum(chip_next + CHIP_ITEMS[2], chip_all)
    chip_items(chip_next, chip_last)
    gather_second("att")
    for s in (XP, ZM, ZP):
        arrived("att", s, 1)
    projects((XP, ZM, ZP))
    chip_more = jnp.minimum(chip_last + CHIP_ITEMS[3], chip_all)
    chip_items(chip_last, chip_more)
    plane_done = jnp.minimum(guest_items, PLANE_ITEMS[0])
    plane_items(0, plane_done)
    gather_third("att")
    chip_most = jnp.minimum(chip_more + CHIP_ITEMS[4], chip_all)
    chip_items(chip_more, chip_most)
    plane_next = jnp.minimum(guest_items, PLANE_ITEMS[1])
    plane_items(plane_done, plane_next)
    for s in (ZZ, ZMX, ZPX, ZZX):
        arrived("att", s, 1)
    projects((ZZ, ZMX, ZPX, ZZX))
    guests_in(2, GUESTS)
    chip_items(chip_most, chip_all)

    @pl.when(z < 2)
    def _():
        def step(k, _):
            finish(own_base + k)
            own_out(k).start()
            return 0

        lax.fori_loop(0, own_count, step, 0)

    plane_items(plane_next, items)

    own_part = pltpu.make_async_copy(
        part.at[pl.ds(pl.multiple_of(head * 128, 128), 128)],
        landed.at[pl.ds(pl.multiple_of(head * 128, 128), 128)],
        in_sem.at[0],
    )
    own_part.start()
    own_part.wait()
    for away in range(1, 8):
        other = (head + away) % 8
        there = landed.at[pl.ds(pl.multiple_of(other * 128, 128), 128)]
        pltpu.make_async_remote_copy(
            src_ref=there, dst_ref=there, send_sem=rs_sem.at[0, 0],
            recv_sem=rs_sem.at[1, other], device_id={"head": other}, device_id_type=MESH,
        ).wait_recv()

    for arguments in sends:
        sent(*arguments).wait_send()
    for k in range(1, 8):
        rs_copy((head + k) % 8, (head + k) % 8).wait_send()
    for k in range(GUESTS):
        @pl.when(k < given)
        def _(k=k):
            guest_q(k).wait_send()
            give_back(k).wait_recv()

        @pl.when(k < guests)
        def _(k=k):
            give_back(k).wait_send()
    for k in range(CHUNKS):
        @pl.when(k < own_count)
        def _(k=k):
            own_out(k).wait()


def last_kernel(rows_hbm, parts_hbm, out_hbm, dec_ref, rows, parts, row_sem, part_sem, out_sem):
    def here(k, count):
        return pl.ds(k * count, count)

    loads = [
        pltpu.make_async_copy(
            rows_hbm.at[here(k, CHUNK)], rows.at[here(k, CHUNK)], row_sem.at[k]
        )
        for k in range(8)
    ]
    adds = [
        pltpu.make_async_copy(
            parts_hbm.at[here(k, 128)], parts.at[here(k, 128)], part_sem.at[k]
        )
        for k in range(8)
    ]
    stores = [
        pltpu.make_async_copy(
            rows.at[here(k, CHUNK)], out_hbm.at[here(k, CHUNK)], out_sem.at[k]
        )
        for k in range(8)
    ]
    for copy in adds + loads:
        copy.start()
    total = jnp.zeros((128, 512), F32)
    for k in range(8):
        adds[k].wait()
        total = total + parts[k * 128:(k + 1) * 128, :].astype(F32)
    dec_ref[...] = total.astype(BF16)
    for k in range(8):
        loads[k].wait()
        stores[k].start()
    for copy in stores:
        copy.wait()


def on_device(prefix_query, prefix_kv, decode_query, tail_key_value, tail_len, out_weight):
    any_space = pl.BlockSpec(memory_space=pl.ANY)
    rows_out, parts = pl.pallas_call(
        kernel,
        out_shape=(
            jax.ShapeDtypeStruct((CHUNKS * CHUNK, WIDTH), BF16),
            jax.ShapeDtypeStruct((1024, 512), BF16),
        ),
        in_specs=[any_space] * 4 + [pl.BlockSpec(memory_space=pltpu.SMEM), any_space],
        out_specs=(any_space, any_space),
        scratch_shapes=[
            pltpu.VMEM((2 * BLOCK, WIDTH), BF16),
            pltpu.VMEM((16 * BLOCK, WIDTH), BF16),
            pltpu.VMEM((16 * BLOCK, WIDTH), BF16),
            pltpu.VMEM((SLOTS * CHUNK, WIDTH), BF16),
            pltpu.VMEM((64 * 256, WIDTH), BF16),
            pltpu.VMEM((1024, 512), BF16),
            pltpu.VMEM((SLOTS * CHUNK, WIDTH), F32),
            pltpu.VMEM((SLOTS * CHUNK, WIDTH), F32),
            pltpu.VMEM((SLOTS * CHUNK, WIDTH), F32),
            pltpu.VMEM((SLOTS * CHUNK, WIDTH), BF16),
            pltpu.VMEM((CHUNK, WIDTH), F32),
            pltpu.VMEM((CHUNK, WIDTH), jnp.int32),
            pltpu.VMEM((1024, 1024), BF16),
            pltpu.VMEM((1024, 512), BF16),
            pltpu.SemaphoreType.DMA((4,)),
            pltpu.SemaphoreType.DMA((CHUNKS,)),
            pltpu.SemaphoreType.DMA((64,)),
            pltpu.SemaphoreType.DMA((8, 2, 2)),
            pltpu.SemaphoreType.DMA((8, 2, 2)),
            pltpu.SemaphoreType.DMA((2, GUESTS)),
            pltpu.SemaphoreType.DMA((2, GUESTS)),
            pltpu.SemaphoreType.DMA((2, 8)),
            pltpu.SemaphoreType.DMA((CHUNKS,)),
        ],
        compiler_params=pltpu.CompilerParams(
            collective_id=0, has_side_effects=True, vmem_limit_bytes=56 << 20
        ),
        name="layer_attention",
    )(
        prefix_query.reshape(CHUNKS * CHUNK, WIDTH),
        prefix_kv.reshape(2 * BLOCK, WIDTH),
        decode_query.reshape(CHUNK, WIDTH),
        tail_key_value.reshape(64 * 256, WIDTH),
        tail_len,
        out_weight,
    )
    prefix_out, decoded = pl.pallas_call(
        last_kernel,
        out_shape=(
            jax.ShapeDtypeStruct((CHUNKS * CHUNK, WIDTH), BF16),
            jax.ShapeDtypeStruct((128, 512), BF16),
        ),
        in_specs=[pl.BlockSpec(memory_space=pltpu.HBM)] * 2,
        out_specs=(pl.BlockSpec(memory_space=pltpu.HBM), pl.BlockSpec(memory_space=pltpu.VMEM)),
        scratch_shapes=[
            pltpu.VMEM((CHUNKS * CHUNK, WIDTH), BF16),
            pltpu.VMEM((1024, 512), BF16),
            pltpu.SemaphoreType.DMA((8,)),
            pltpu.SemaphoreType.DMA((8,)),
            pltpu.SemaphoreType.DMA((8,)),
        ],
        compiler_params=pltpu.CompilerParams(vmem_limit_bytes=56 << 20),
        name="results",
    )(rows_out, parts)
    return prefix_out.reshape(prefix_query.shape), decoded


def solution(mesh):
    return jax.shard_map(
        on_device,
        mesh=mesh,
        in_specs=(
            P(("ctx", "rep"), "head", None),
            P(("ctx", "rep"), "head", None, None),
            P(("ctx", "rep"), "head", None),
            P(("ctx", "rep"), None, "head", None, None),
            P(("ctx", "rep")),
            P("head", ("ctx", "rep")),
        ),
        out_specs=(P(("ctx", "rep"), "head", None), P("head", ("ctx", "rep"))),
        check_vma=False,
    )
```

```python
import functools

import jax
import jax.numpy as jnp
from jax import lax
from jax.experimental import pallas as pl
from jax.experimental.pallas import tpu as pltpu
from jax.sharding import PartitionSpec as P

F32, BF16 = jnp.float32, jnp.bfloat16
MESH = pl.DeviceIdType.MESH
LOW_FILL = -1e30
WIDTH = 128
SCALE = WIDTH**-0.5 * 1.4426950408889634
BLOCK = 512
CHUNK = 512
CHUNKS = 8
GUESTS = 4
GUEST_BASE = 1 + CHUNKS
SLOTS = 1 + CHUNKS + GUESTS + 1
NT = (((1,), (1,)), ((), ()))
EARLY = 1
ROLLS = 16
CHIP_ITEMS = (1, 2, 2, 1, 1)
PLANE_ITEMS = (1, 3)


def wide(column, width):
    return jnp.concatenate([column] * (width // WIDTH), axis=1)


def kernel(
    q_hbm, kv_hbm, dq_hbm, tail_hbm, len_ref, w_hbm,
    out_hbm, landed,
    kvint, kbuf, vbuf, qbuf, tailbuf, wbuf, m_ref, l_ref, acc_ref,
    obuf, fbuf, ahead, att, part,
    in_sem, q_sem, send_sem, kv_sem, att_sem, guest_sem, back_sem, rs_sem, out_sem,
):
    ctx, head, rep = lax.axis_index("ctx"), lax.axis_index("head"), lax.axis_index("rep")
    z, x = ctx // 2, ctx % 2
    me = ctx * 2 + rep
    mate = 15 - me
    late = me >= 8
    def shared(i):
        return (i - 7) * 7 // 16

    guests = jnp.where(late, 0, shared(mate))
    given = jnp.where(late, shared(me), 0)
    own_base = 1
    own_count = CHUNKS - given

    def place(dz, flip):
        return ((z + dz) % 4) * 2 + (1 - x if flip else x)

    chips = [ctx, place(0, True), place(1, False), place(3, False),
             place(1, True), place(3, True), place(2, False), place(2, True)]
    OWN, XP, ZP, ZM, ZPX, ZMX, ZZ, ZZX = range(8)

    sibling = {"ctx": ctx, "rep": 1 - rep}
    over_x = {"ctx": chips[XP], "rep": rep}
    over_zp = {"ctx": chips[ZP], "rep": rep}
    over_zm = {"ctx": chips[ZM], "rep": rep}
    to_mate = {"ctx": mate // 2, "rep": mate % 2}

    barrier = pltpu.get_barrier_semaphore()
    for device in (sibling, over_x, over_zp, over_zm, to_mate):
        pl.semaphore_signal(barrier, inc=1, device_id=device, device_id_type=MESH)
    for away in range(1, 8):
        pl.semaphore_signal(
            barrier, inc=1, device_id={"head": (head + away) % 8}, device_id_type=MESH
        )

    def load(src, dst, sem):
        copy = pltpu.make_async_copy(src, dst, sem)
        copy.start()
        return copy

    kv_in = load(kv_hbm, kvint, in_sem.at[0])
    dq_in = load(dq_hbm, qbuf.at[pl.ds(0, CHUNK)], in_sem.at[1])

    def own_q(k):
        return pltpu.make_async_copy(
            q_hbm.at[pl.ds(pl.multiple_of((given + k) * CHUNK, CHUNK), CHUNK)],
            qbuf.at[pl.ds(pl.multiple_of((own_base + k) * CHUNK, CHUNK), CHUNK)],
            q_sem.at[k],
        )

    for k in range(CHUNKS):
        @pl.when(k < own_count)
        def _(k=k):
            own_q(k).start()

    tail_in = load(tail_hbm, tailbuf, in_sem.at[2])
    w_in = load(w_hbm, wbuf, in_sem.at[3])

    rows = lax.broadcasted_iota(jnp.int32, (256, 256), 0)
    cols = lax.broadcasted_iota(jnp.int32, (256, 256), 1)
    wanted = jnp.where(rows < 128, rows * 2, (rows - 128) * 2 + 1)
    pick = jnp.where(cols == wanted, 1.0, 0.0).astype(BF16)
    kv_in.wait()
    for t in range(4):
        apart = jnp.dot(pick, kvint[t * 256:(t + 1) * 256, :], preferred_element_type=F32)
        apart = apart.astype(BF16)
        here = pl.ds(pl.multiple_of(me * BLOCK + t * 128, 128), 128)
        kbuf[here, :] = apart[:128]
        vbuf[here, :] = apart[128:]

    m_ref[...] = jnp.full(m_ref.shape, LOW_FILL, F32)
    l_ref[...] = jnp.zeros(l_ref.shape, F32)
    acc_ref[...] = jnp.zeros(acc_ref.shape, F32)
    ahead[...] = (
        lax.broadcasted_iota(jnp.int32, (CHUNK, WIDTH), 1)
        - lax.broadcasted_iota(jnp.int32, (CHUNK, WIDTH), 0) // 8
    )
    pl.semaphore_wait(barrier, 12)

    sends = []

    def block_of(which, s, kind, piece):
        b = chips[s] * 2 + (rep if kind == 0 else 1 - rep)
        if which == "kv":
            ref = kbuf if piece == 0 else vbuf
            return ref.at[pl.ds(pl.multiple_of(b * BLOCK, BLOCK), BLOCK)]
        return att.at[pl.ds(pl.multiple_of(b * 64 + piece * 32, 32), 32)]

    def sem_of(which):
        return kv_sem if which == "kv" else att_sem

    def send(which, s, piece, device, s_there, kind_there):
        arguments = (which, s, piece, device, s_there, kind_there, len(sends))
        sends.append(arguments)
        sent(*arguments).start()

    def sent(which, s, piece, device, s_there, kind_there, number):
        return pltpu.make_async_remote_copy(
            src_ref=block_of(which, s, 0, piece),
            dst_ref=block_of(which, s, 0, piece),
            send_sem=send_sem.at[number],
            recv_sem=sem_of(which).at[s_there, kind_there, piece],
            device_id=device,
            device_id_type=MESH,
        )

    def arrived(which, s, kind, pieces=(0, 1)):
        for piece in pieces:
            ref = block_of(which, s, kind, piece)
            pltpu.make_async_remote_copy(
                src_ref=ref, dst_ref=ref, send_sem=send_sem.at[0],
                recv_sem=sem_of(which).at[s, kind, piece],
                device_id=sibling, device_id_type=MESH,
            ).wait_recv()

    def both(which, s, device, s_there, kind_there):
        for piece in (0, 1):
            send(which, s, piece, device, s_there, kind_there)

    def gather_start(which):
        both(which, OWN, over_zp, ZM, 0)
        both(which, OWN, over_zm, ZP, 0)
        both(which, OWN, over_x, XP, 0)
        both(which, OWN, sibling, OWN, 1)

    def gather_first(which):
        arrived(which, ZM, 0)
        send(which, ZM, 0, over_zp, ZZ, 0)
        arrived(which, ZP, 0)
        send(which, ZP, 1, over_zm, ZZ, 0)
        arrived(which, XP, 0)
        both(which, XP, over_zp, ZMX, 0)
        both(which, XP, over_zm, ZPX, 0)
        for s in (XP, ZM, ZP):
            both(which, s, sibling, s, 1)

    def gather_second(which):
        arrived(which, ZZ, 0)
        both(which, ZZ, over_x, ZZX, 0)
        both(which, ZZ, sibling, ZZ, 1)

    def gather_third(which):
        for s in (ZMX, ZPX, ZZX):
            arrived(which, s, 0)
            both(which, s, sibling, s, 1)

    gather_start("kv")

    def guest_q(k):
        return pltpu.make_async_remote_copy(
            src_ref=q_hbm.at[pl.ds(pl.multiple_of(k * CHUNK, CHUNK), CHUNK)],
            dst_ref=qbuf.at[pl.ds(pl.multiple_of((GUEST_BASE + k) * CHUNK, CHUNK), CHUNK)],
            send_sem=guest_sem.at[0, k], recv_sem=guest_sem.at[1, k],
            device_id=to_mate, device_id_type=MESH,
        )

    def rows_of(slot):
        return pl.ds(pl.multiple_of(slot * CHUNK, CHUNK), CHUNK)

    def absorb(slots, ranges, seen=None):
        where = [rows_of(slot) for slot in slots]
        keys = [pl.ds(pl.multiple_of(first, BLOCK), count) for first, count in ranges]
        old = [(m_ref[r, :], l_ref[r, :], acc_ref[r, :]) for r in where]
        scores = [
            [lax.dot_general(qbuf[r, :], kbuf[k, :], NT, preferred_element_type=F32) for k in keys]
            for r in where
        ]
        result = []
        for i, (m_old, l_old, a_old) in enumerate(old):
            parts = scores[i]
            if seen is not None:
                parts = [
                    jnp.concatenate(
                        [
                            jnp.where(
                                ahead[...] <= seen[i] - j * WIDTH,
                                s[:, j * WIDTH:(j + 1) * WIDTH],
                                LOW_FILL,
                            )
                            for j in range(s.shape[1] // WIDTH)
                        ],
                        axis=1,
                    )
                    for s in parts
                ]
            m_new = functools.reduce(
                jnp.maximum, [jnp.max(s, axis=1, keepdims=True) for s in parts], m_old
            )
            factor = jnp.exp2((m_old - m_new) * SCALE)
            total, mixed = l_old * factor, a_old * factor
            for s, k in zip(parts, keys):
                p = jnp.exp2((s - wide(m_new, s.shape[1])) * SCALE)
                for j in range(s.shape[1] // WIDTH):
                    total = total + p[:, j * WIDTH:(j + 1) * WIDTH]
                mixed = mixed + jnp.dot(p.astype(BF16), vbuf[k, :], preferred_element_type=F32)
            result.append((m_new, total, mixed))
        for i, r in enumerate(where):
            m_ref[r, :], l_ref[r, :], acc_ref[r, :] = result[i]

    def first_items(slot, lo, hi, who, place):
        blocks = who % 2 + 1

        def step(t, _):
            pair, b = t // blocks, t % blocks
            last = b == blocks - 1
            seen = [
                jnp.where(last, (place + 2 * pair + i) * 64, 2 * BLOCK) for i in range(2)
            ]
            absorb(
                [slot + 2 * pair, slot + 2 * pair + 1],
                [((who - blocks + 1 + b) * BLOCK, BLOCK)],
                seen,
            )
            return 0

        lax.fori_loop(lo * blocks, hi * blocks, step, 0)

    def half_items(slot, lo, hi, who):
        def step(k, _):
            absorb([slot + k], [(who // 4 * 4 * BLOCK, 2 * BLOCK)])
            return 0

        lax.fori_loop(lo, jnp.where(who // 2 % 2 == 1, hi, lo), step, 0)

    before = jnp.where(z > 0, 1, 0)
    own_pairs = (own_count + 1) // 2
    chip_early = own_pairs * (x + before)
    chip_all = chip_early + own_pairs * before

    def chip_items(lo, hi):
        def step(t, _):
            b, k = t // own_pairs, t % own_pairs
            chip = jnp.where(
                jnp.logical_and(x == 1, b == 0),
                chips[XP],
                jnp.where(b == x, chips[ZM], chips[ZMX]),
            )
            absorb([own_base + 2 * k, own_base + 2 * k + 1], [(chip * 2 * BLOCK, 2 * BLOCK)])
            return 0

        lax.fori_loop(lo, hi, step, 0)

    def pick_chip(k, group):
        return functools.reduce(
            lambda rest, n: jnp.where(k == n, chips[group[n]], rest),
            range(1, len(group)),
            chips[group[0]],
        )

    def decode_items(first, second):
        def step(k, _):
            where = (pick_chip(k, first), pick_chip(k, second))
            absorb([0], [(chip * 2 * BLOCK, 2 * BLOCK) for chip in where])
            return 0

        lax.fori_loop(0, 2, step, 0)

    def finish(slot):
        r = rows_of(slot)
        obuf[r, :] = (
            acc_ref[r, :] / jnp.sum(l_ref[r, :], axis=1, keepdims=True)
        ).astype(BF16)

    def own_out(k):
        return pltpu.make_async_copy(
            obuf.at[pl.ds(pl.multiple_of((own_base + k) * CHUNK, CHUNK), CHUNK)],
            out_hbm.at[pl.ds(pl.multiple_of((given + k) * CHUNK, CHUNK), CHUNK)],
            out_sem.at[k],
        )

    def give(lo, hi):
        for k in range(lo, hi):
            @pl.when(k < given)
            def _(k=k):
                guest_q(k).start()

    dq_in.wait()
    tail_in.wait()

    def tail_step(t, _):
        first = t * ROLLS
        scores, kv = [], []
        col = lax.broadcasted_iota(jnp.int32, (8, 256), 1)
        even = jnp.where(col % 2 == 0, col, 512)
        for u in range(ROLLS):
            r = first + u
            kv.append(pl.ds(pl.multiple_of(r * 256, 256), 256))
            q16 = qbuf[pl.ds(pl.multiple_of((first + u // 2 * 2) * 8, 16), 16), :]
            s = lax.dot_general(q16, tailbuf[kv[u], :], NT, preferred_element_type=F32)
            s = s[u % 2 * 8:u % 2 * 8 + 8]
            scores.append(jnp.where(even < 2 * len_ref[r], s, LOW_FILL))
        s = jnp.concatenate(scores, axis=0)
        m_new = jnp.broadcast_to(jnp.max(s, axis=1, keepdims=True), (8 * ROLLS, WIDTH))
        p = jnp.exp2((s - wide(m_new, 256)) * SCALE)
        here = pl.ds(pl.multiple_of(t * 8 * ROLLS, 8 * ROLLS), 8 * ROLLS)
        m_ref[here, :] = m_new
        l_ref[here, :] = p[:, :WIDTH] + p[:, WIDTH:]
        p = pltpu.roll(p, 1, 1).astype(BF16)
        out = []
        for u in range(ROLLS):
            p16 = p[u // 2 * 16:u // 2 * 16 + 16]
            o = jnp.dot(p16, tailbuf[kv[u], :], preferred_element_type=F32)
            out.append(o[u % 2 * 8:u % 2 * 8 + 8])
        acc_ref[here, :] = jnp.concatenate(out, axis=0)
        return 0

    lax.fori_loop(0, 64 // ROLLS, tail_step, 0)

    arrived("kv", OWN, 1)
    for k in range(CHUNKS):
        @pl.when(k < own_count)
        def _(k=k):
            own_q(k).wait()

    first_items(own_base, 0, 1, me, given)
    gather_first("kv")
    first_items(own_base, 1, own_pairs, me, given)
    gather_second("kv")
    give(0, EARLY)
    for s in (XP, ZM, ZP):
        arrived("kv", s, 1)
    decode_items((OWN, ZM), (XP, ZP))
    chip_done = jnp.minimum(chip_early, CHIP_ITEMS[0])
    chip_items(0, chip_done)
    gather_third("kv")
    give(EARLY, GUESTS)
    for s in (ZZ, ZMX, ZPX, ZZX):
        arrived("kv", s, 1)
    decode_items((ZZ, ZPX), (ZMX, ZZX))

    total = jnp.sum(l_ref[:CHUNK, :], axis=1, keepdims=True)
    fbuf[...] = acc_ref[:CHUNK, :] / total
    mine = pl.ds(pl.multiple_of(me * 64, 64), 64)
    for h in range(8):
        att[mine, h * WIDTH:(h + 1) * WIDTH] = fbuf[pl.ds(h, 64, stride=8), :].astype(BF16)
    gather_start("att")

    def rs_copy(chip, number):
        return pltpu.make_async_remote_copy(
            src_ref=part.at[pl.ds(pl.multiple_of(chip * 128, 128), 128)],
            dst_ref=landed.at[pl.ds(pl.multiple_of(head * 128, 128), 128)],
            send_sem=rs_sem.at[0, number], recv_sem=rs_sem.at[1, head],
            device_id={"head": chip}, device_id_type=MESH,
        )

    def project(chip):
        rows_here = pl.ds(pl.multiple_of(chip * 128, 128), 128)
        part[rows_here, :] = jnp.dot(
            att[rows_here, :], wbuf[...], preferred_element_type=F32
        ).astype(BF16)

        @pl.when(chip != head)
        def _():
            rs_copy(chip, chip).start()

    def give_back(k):
        return pltpu.make_async_remote_copy(
            src_ref=obuf.at[pl.ds(pl.multiple_of((GUEST_BASE + k) * CHUNK, CHUNK), CHUNK)],
            dst_ref=out_hbm.at[pl.ds(pl.multiple_of(k * CHUNK, CHUNK), CHUNK)],
            send_sem=back_sem.at[0, k], recv_sem=back_sem.at[1, k],
            device_id=to_mate, device_id_type=MESH,
        )

    def projects(group):
        def step(k, _):
            project(pick_chip(k, group))
            return 0

        lax.fori_loop(0, len(group), step, 0)

    guest_planes, own_planes = mate // 4, jnp.maximum(z - 1, 0)
    guest_items = guests * guest_planes
    items = guest_items + own_count * own_planes

    def plane_items(lo, hi):
        def step(t, _):
            foreign = t < guest_items
            after = jnp.where(foreign, t, t - guest_items)
            planes = jnp.maximum(jnp.where(foreign, guest_planes, own_planes), 1)
            k, j = after // planes, after % planes
            slot = jnp.where(foreign, GUEST_BASE, own_base) + k
            absorb([slot], [(j * 4 * BLOCK, 4 * BLOCK)])

            @pl.when(j == planes - 1)
            def _():
                finish(slot)

                @pl.when(foreign)
                def _():
                    give_back(k).start()

                @pl.when(jnp.logical_not(foreign))
                def _():
                    own_out(k).start()

            return 0

        lax.fori_loop(lo, hi, step, 0)

    w_in.wait()
    chip_next = jnp.minimum(chip_done + CHIP_ITEMS[1], chip_all)
    chip_items(chip_done, chip_next)
    arrived("att", OWN, 1)
    project(ctx)
    gather_first("att")

    def guest_in(k, _):
        guest_q(k).wait_recv()
        return 0

    def guests_in(lo, hi):
        hi = jnp.minimum(hi, guests)
        lax.fori_loop(lo, hi, guest_in, 0)
        first_items(GUEST_BASE, lo // 2, (hi + 1) // 2, mate, 0)
        half_items(GUEST_BASE, lo, hi, mate)

    guests_in(0, 2)
    chip_last = jnp.minimum(chip_next + CHIP_ITEMS[2], chip_all)
    chip_items(chip_next, chip_last)
    gather_second("att")
    for s in (XP, ZM, ZP):
        arrived("att", s, 1)
    projects((XP, ZM, ZP))
    chip_more = jnp.minimum(chip_last + CHIP_ITEMS[3], chip_all)
    chip_items(chip_last, chip_more)
    plane_done = jnp.minimum(guest_items, PLANE_ITEMS[0])
    plane_items(0, plane_done)
    gather_third("att")
    chip_most = jnp.minimum(chip_more + CHIP_ITEMS[4], chip_all)
    chip_items(chip_more, chip_most)
    plane_next = jnp.minimum(guest_items, PLANE_ITEMS[1])
    plane_items(plane_done, plane_next)
    for s in (ZZ, ZMX, ZPX, ZZX):
        arrived("att", s, 1)
    projects((ZZ, ZMX, ZPX, ZZX))
    guests_in(2, GUESTS)
    chip_items(chip_most, chip_all)

    @pl.when(z < 2)
    def _():
        def step(k, _):
            finish(own_base + k)
            own_out(k).start()
            return 0

        lax.fori_loop(0, own_count, step, 0)

    plane_items(plane_next, items)

    own_part = pltpu.make_async_copy(
        part.at[pl.ds(pl.multiple_of(head * 128, 128), 128)],
        landed.at[pl.ds(pl.multiple_of(head * 128, 128), 128)],
        in_sem.at[0],
    )
    own_part.start()
    own_part.wait()
    for away in range(1, 8):
        other = (head + away) % 8
        there = landed.at[pl.ds(pl.multiple_of(other * 128, 128), 128)]
        pltpu.make_async_remote_copy(
            src_ref=there, dst_ref=there, send_sem=rs_sem.at[0, 0],
            recv_sem=rs_sem.at[1, other], device_id={"head": other}, device_id_type=MESH,
        ).wait_recv()

    for arguments in sends:
        sent(*arguments).wait_send()
    for k in range(1, 8):
        rs_copy((head + k) % 8, (head + k) % 8).wait_send()
    for k in range(GUESTS):
        @pl.when(k < given)
        def _(k=k):
            guest_q(k).wait_send()
            give_back(k).wait_recv()

        @pl.when(k < guests)
        def _(k=k):
            give_back(k).wait_send()
    for k in range(CHUNKS):
        @pl.when(k < own_count)
        def _(k=k):
            own_out(k).wait()


def last_kernel(rows_hbm, parts_hbm, out_hbm, dec_ref, rows, parts, row_sem, part_sem, out_sem):
    def here(k, count):
        return pl.ds(k * count, count)

    loads = [
        pltpu.make_async_copy(
            rows_hbm.at[here(k, CHUNK)], rows.at[here(k, CHUNK)], row_sem.at[k]
        )
        for k in range(8)
    ]
    adds = [
        pltpu.make_async_copy(
            parts_hbm.at[here(k, 128)], parts.at[here(k, 128)], part_sem.at[k]
        )
        for k in range(8)
    ]
    stores = [
        pltpu.make_async_copy(
            rows.at[here(k, CHUNK)], out_hbm.at[here(k, CHUNK)], out_sem.at[k]
        )
        for k in range(8)
    ]
    for copy in adds + loads:
        copy.start()
    total = jnp.zeros((128, 512), F32)
    for k in range(8):
        adds[k].wait()
        total = total + parts[k * 128:(k + 1) * 128, :].astype(F32)
    dec_ref[...] = total.astype(BF16)
    for k in range(8):
        loads[k].wait()
        stores[k].start()
    for copy in stores:
        copy.wait()


def on_device(prefix_query, prefix_kv, decode_query, tail_key_value, tail_len, out_weight):
    any_space = pl.BlockSpec(memory_space=pl.ANY)
    rows_out, parts = pl.pallas_call(
        kernel,
        out_shape=(
            jax.ShapeDtypeStruct((CHUNKS * CHUNK, WIDTH), BF16),
            jax.ShapeDtypeStruct((1024, 512), BF16),
        ),
        in_specs=[any_space] * 4 + [pl.BlockSpec(memory_space=pltpu.SMEM), any_space],
        out_specs=(any_space, any_space),
        scratch_shapes=[
            pltpu.VMEM((2 * BLOCK, WIDTH), BF16),
            pltpu.VMEM((16 * BLOCK, WIDTH), BF16),
            pltpu.VMEM((16 * BLOCK, WIDTH), BF16),
            pltpu.VMEM((SLOTS * CHUNK, WIDTH), BF16),
            pltpu.VMEM((64 * 256, WIDTH), BF16),
            pltpu.VMEM((1024, 512), BF16),
            pltpu.VMEM((SLOTS * CHUNK, WIDTH), F32),
            pltpu.VMEM((SLOTS * CHUNK, WIDTH), F32),
            pltpu.VMEM((SLOTS * CHUNK, WIDTH), F32),
            pltpu.VMEM((SLOTS * CHUNK, WIDTH), BF16),
            pltpu.VMEM((CHUNK, WIDTH), F32),
            pltpu.VMEM((CHUNK, WIDTH), jnp.int32),
            pltpu.VMEM((1024, 1024), BF16),
            pltpu.VMEM((1024, 512), BF16),
            pltpu.SemaphoreType.DMA((4,)),
            pltpu.SemaphoreType.DMA((CHUNKS,)),
            pltpu.SemaphoreType.DMA((64,)),
            pltpu.SemaphoreType.DMA((8, 2, 2)),
            pltpu.SemaphoreType.DMA((8, 2, 2)),
            pltpu.SemaphoreType.DMA((2, GUESTS)),
            pltpu.SemaphoreType.DMA((2, GUESTS)),
            pltpu.SemaphoreType.DMA((2, 8)),
            pltpu.SemaphoreType.DMA((CHUNKS,)),
        ],
        compiler_params=pltpu.CompilerParams(
            collective_id=0, has_side_effects=True, vmem_limit_bytes=56 << 20
        ),
        name="layer_attention",
    )(
        prefix_query.reshape(CHUNKS * CHUNK, WIDTH),
        prefix_kv.reshape(2 * BLOCK, WIDTH),
        decode_query.reshape(CHUNK, WIDTH),
        tail_key_value.reshape(64 * 256, WIDTH),
        tail_len,
        out_weight,
    )
    prefix_out, decoded = pl.pallas_call(
        last_kernel,
        out_shape=(
            jax.ShapeDtypeStruct((CHUNKS * CHUNK, WIDTH), BF16),
            jax.ShapeDtypeStruct((128, 512), BF16),
        ),
        in_specs=[pl.BlockSpec(memory_space=pltpu.HBM)] * 2,
        out_specs=(pl.BlockSpec(memory_space=pltpu.HBM), pl.BlockSpec(memory_space=pltpu.VMEM)),
        scratch_shapes=[
            pltpu.VMEM((CHUNKS * CHUNK, WIDTH), BF16),
            pltpu.VMEM((1024, 512), BF16),
            pltpu.SemaphoreType.DMA((8,)),
            pltpu.SemaphoreType.DMA((8,)),
            pltpu.SemaphoreType.DMA((8,)),
        ],
        compiler_params=pltpu.CompilerParams(vmem_limit_bytes=56 << 20),
        name="results",
    )(rows_out, parts)
    return prefix_out.reshape(prefix_query.shape), decoded


def solution(mesh):
    return jax.shard_map(
        on_device,
        mesh=mesh,
        in_specs=(
            P(("ctx", "rep"), "head", None),
            P(("ctx", "rep"), "head", None, None),
            P(("ctx", "rep"), "head", None),
            P(("ctx", "rep"), None, "head", None, None),
            P(("ctx", "rep")),
            P("head", ("ctx", "rep")),
        ),
        out_specs=(P(("ctx", "rep"), "head", None), P("head", ("ctx", "rep"))),
        check_vma=False,
    )
```
